32 devices in a mesh: dp: 8 (over y, x, core), tensor: 4 (over z).
Axes of the slice: x: 2, y: 2, z: 4, core: 2. Of those that a mesh axis runs over, the one named last changes fastest.
Arguments:
- tokens: bfloat16 [16, 1024, 768], P('dp', 'tensor'), may hold values from -6 to 6
- segment_ids: int32 [16, 1024], P('dp'), may hold values from 0 to 1023, as said below
- gain_first: float32 [768], replicated, may hold values from 0.5 to 1.5
- shift_first: float32 [768], replicated, may hold values from -3 to 3
- weight_qkv: bfloat16 [768, 3, 768], P(None, None, 'tensor'), may hold values from -0.21875 to 0.21875
- bias_qv: float32 [2, 768], P(None, 'tensor'), may hold values from -3 to 3
- weight_out: bfloat16 [768, 768], P('tensor'), may hold values from -0.625 to 0.625
- bias_out: float32 [768], replicated, may hold values from -3 to 3
- gain_second: float32 [768], replicated, may hold values from 0.5 to 1.5
- shift_second: float32 [768], replicated, may hold values from -3 to 3
- weight_up: bfloat16 [768, 3072], P(None, 'tensor'), may hold values from -0.21875 to 0.21875
- bias_up: float32 [3072], P('tensor'), may hold values from -3 to 3
- weight_down: bfloat16 [3072, 768], P('tensor'), may hold values from -0.15625 to 0.15625
- bias_down: float32 [768], replicated, may hold values from -3 to 3
- cotangent: bfloat16 [16, 1024, 768], P('dp', 'tensor'), may hold values from -6 to 6
Outputs:
- block_out: bfloat16 [16, 1024, 768], P('dp', 'tensor')
- input_grad: float32 [16, 1024, 768], P('dp', 'tensor')
- gain_first_grad: float32 [768], replicated
- shift_first_grad: float32 [768], replicated
- weight_qkv_grad: float32 [768, 3, 768], P(None, None, 'tensor')
- bias_qv_grad: float32 [2, 768], P(None, 'tensor')
- weight_out_grad: float32 [768, 768], P('tensor')
- bias_out_grad: float32 [768], replicated
- gain_second_grad: float32 [768], replicated
- shift_second_grad: float32 [768], replicated
- weight_up_grad: float32 [768, 3072], P(None, 'tensor')
- bias_up_grad: float32 [3072], P('tensor')
- weight_down_grad: float32 [3072, 768], P('tensor')
- bias_down_grad: float32 [768], replicated
The draws below stay inside these ranges and needn't reach their ends.
Inputs may be any that keep to these rules, and one draw needn't show every extreme that they name: `segment_ids`: along each row the ids start at 0, never fall, and rise by at most one from one position to the next. In each aligned block of 2 rows one row is a single cell, and in some row every position is a cell of its own.
All inputs are finite; a program needn't handle non-finite values.
Results may differ from the reference program's by a relative error of at most 0.018.
Values may be sent and summed in bfloat16 or wider, within the bound.
A program may use at most 128 MiB of HBM per device.

```python
import jax
import jax.numpy as jnp
from jax import lax

D = 768
HEADS = 12
HEAD = 64
FF = 3072
SEQ = 1024
MICRO = 2
ROWS = 16


def draw_segment_ids(key, part):
    key = jax.random.fold_in(key, 7)
    key_len, key_top, key_single, key_rise = jax.random.split(key, 4)
    shortest = max(2, SEQ // 64)
    count = SEQ // shortest
    tops = jnp.array([SEQ // 16, SEQ // 8, SEQ // 4], jnp.int32)
    row_top = tops[jax.random.randint(key_top, (ROWS, 1), 0, 3)]
    lengths = jax.random.randint(key_len, (ROWS, count), shortest, row_top + 1).astype(jnp.int32)
    ends = jnp.cumsum(lengths, axis=1).astype(jnp.int32)
    places = jnp.arange(SEQ, dtype=jnp.int32)
    ids = jnp.sum((ends[:, None, :] <= places[None, :, None]).astype(jnp.int32), axis=2)
    blocks = ROWS // MICRO
    single_slot = jax.random.randint(key_single, (blocks,), 0, MICRO).astype(jnp.int32)
    rows = jnp.arange(ROWS, dtype=jnp.int32)
    single_row = rows % MICRO == jnp.repeat(single_slot, MICRO)
    rise_block = jax.random.randint(key_rise, (), 0, blocks).astype(jnp.int32)
    rise_slot = (single_slot[rise_block] + 1) % MICRO
    rise_row = rows == rise_block * MICRO + rise_slot
    ids = jnp.where(single_row[:, None], 0, ids)
    ids = jnp.where(rise_row[:, None], places[None, :], ids)
    return ids.astype(jnp.int32)


def shard_levels(rng, dims, pieces, smallest, largest):
    def one(position, parts):
        draws = jax.random.uniform(jax.random.fold_in(jax.random.fold_in(rng, 6), position), (parts,), jnp.float32, smallest / len(pieces), largest / len(pieces))
        return jnp.repeat(jnp.exp(draws), dims[position] // parts).reshape((-1,) + (1,) * (len(dims) - position - 1))

    level = one(*pieces[0])
    for cut in pieces[1:]:
        level = level * one(*cut)
    return level


def normal_values(rng, dims, scale, limit, cuts=(), held_as=jnp.bfloat16):
    loudness = shard_levels(rng, dims, cuts, -0.22, 0.18) if cuts else 1.0
    result = jax.random.normal(rng, dims, jnp.float32) * scale * loudness
    return jnp.minimum(jnp.maximum(result, -limit), limit).astype(held_as)


def setup_inputs(seed: int = 0) -> dict:
    keys = jax.random.split(jax.random.key(seed), 16)
    tokens = normal_values(keys[0], (ROWS, SEQ, D), 1.0, 6.0, ((0, 8), (1, 4)))
    segment_ids = draw_segment_ids(jax.random.fold_in(keys[15], 71), 0)
    gain_first = jnp.clip(1.0 + 0.1 * jax.random.normal(keys[2], (D,), jnp.float32), 0.5, 1.5)
    shift_first = normal_values(keys[3], (D,), 0.3, 3.0, (), jnp.float32)
    weight_qkv = normal_values(keys[4], (D, 3, D), D ** -0.5, 0.21875, ((2, 4),))
    bias_qv = normal_values(keys[5], (2, D), 0.3, 3.0, ((1, 4),), jnp.float32)
    weight_out = normal_values(keys[6], (D, D), (D // 8) ** -0.5, 0.625, ((0, 4),))
    bias_out = normal_values(keys[7], (D,), 0.3, 3.0, (), jnp.float32)
    gain_second = jnp.clip(1.0 + 0.1 * jax.random.normal(keys[8], (D,), jnp.float32), 0.5, 1.5)
    shift_second = normal_values(keys[9], (D,), 0.3, 3.0, (), jnp.float32)
    weight_up = normal_values(keys[10], (D, FF), D ** -0.5, 0.21875, ((1, 4),))
    bias_up = normal_values(keys[11], (FF,), 0.3, 3.0, ((0, 4),), jnp.float32)
    weight_down = normal_values(keys[12], (FF, D), (FF // 2) ** -0.5, 0.15625, ((0, 4),))
    bias_down = normal_values(keys[13], (D,), 0.3, 3.0, (), jnp.float32)
    cotangent = normal_values(keys[14], (ROWS, SEQ, D), 1.0, 6.0, ((0, 8), (1, 4)))
    return {"tokens": tokens, "segment_ids": segment_ids, "gain_first": gain_first, "shift_first": shift_first, "weight_qkv": weight_qkv, "bias_qv": bias_qv, "weight_out": weight_out, "bias_out": bias_out, "gain_second": gain_second, "shift_second": shift_second, "weight_up": weight_up, "bias_up": bias_up, "weight_down": weight_down, "bias_down": bias_down, "cotangent": cotangent}


@jax.custom_vjp
def low(v):
    return lax.optimization_barrier(v.astype(jnp.bfloat16)).astype(jnp.float32)

@jax.custom_vjp
def low_back(v):
    return v

def low_keep(v):
    return (low(v), None)

def low_pass(kept, grad):
    return (grad,)

def back_keep(v):
    return (v, None)

def back_low(kept, grad):
    return (low(grad),)
low.defvjp(low_keep, low_pass)
low_back.defvjp(back_keep, back_low)

def layer_norm(inputs, scaling, offset):
    center = inputs - lax.optimization_barrier(jnp.mean(inputs, axis=-1, keepdims=True))
    spread = lax.optimization_barrier(jnp.mean(center * center, axis=-1, keepdims=True))
    return center * lax.rsqrt(spread + 1e-05) * scaling + offset

def block(inputs, id_rows, weights):
    gain_first, shift_first, weight_qkv, bias_qv, weight_out, bias_out, gain_second, shift_second, weight_up, bias_up, weight_down, bias_down = weights
    highest = lax.Precision.HIGHEST
    row_count = inputs.shape[0]
    sent_first = low(layer_norm(inputs, gain_first, shift_first))
    projected = jnp.einsum('rtd,dcj->rtcj', sent_first, weight_qkv, precision=highest)
    queries = low_back(low(projected[:, :, 0] + bias_qv[0])).reshape(row_count, SEQ, HEADS, HEAD)
    keys_low = low_back(low(projected[:, :, 1])).reshape(row_count, SEQ, HEADS, HEAD)
    values_low = low_back(low(projected[:, :, 2] + bias_qv[1])).reshape(row_count, SEQ, HEADS, HEAD)
    raw_scores = low_back(jnp.einsum('rqhd,rkhd->rhqk', queries, keys_low, precision=highest) * HEAD ** (-0.5))
    same_cell = (id_rows[:, :, None] == id_rows[:, None, :])[:, None]
    scores = jnp.where(same_cell, raw_scores, -1e+30)
    log_totals = jax.nn.logsumexp(scores, axis=-1, keepdims=True)
    weights_low = low(jnp.exp(scores - log_totals))
    context = low_back(low(jnp.einsum('rhqk,rkhd->rqhd', weights_low, values_low, precision=highest)))
    context = context.reshape(row_count, SEQ, D)
    attended = jnp.einsum('rtj,jd->rtd', context, weight_out, precision=highest)
    middle = inputs + low_back(attended) + bias_out
    sent_second = low(layer_norm(middle, gain_second, shift_second))
    hidden_pre = low_back(jnp.einsum('rtd,df->rtf', sent_second, weight_up, precision=highest) + bias_up)
    active = low(jax.nn.gelu(hidden_pre, approximate=False))
    fed_forward = jnp.einsum('rtf,fd->rtd', active, weight_down, precision=highest)
    return middle + low_back(fed_forward) + bias_down

def reference(tokens, segment_ids, gain_first, shift_first, weight_qkv, bias_qv, weight_out, bias_out, gain_second, shift_second, weight_up, bias_up, weight_down, bias_down, cotangent):
    params = tuple((argument.astype(jnp.float32) for argument in (gain_first, shift_first, weight_qkv, bias_qv, weight_out, bias_out, gain_second, shift_second, weight_up, bias_up, weight_down, bias_down)))
    row_group = 2

    def forward(inputs, weights):
        grouped = inputs.reshape(ROWS // row_group, row_group, SEQ, D)
        id_groups = segment_ids.reshape(ROWS // row_group, row_group, SEQ)

        def one_group(member):
            return block(member[0], member[1], weights)
        results = lax.map(jax.checkpoint(one_group), (grouped, id_groups))
        return results.reshape(ROWS, SEQ, D)
    outputs, pullback = jax.vjp(forward, tokens.astype(jnp.float32), params)
    input_grad, weight_grads = pullback(cotangent.astype(jnp.float32))
    return (outputs.astype(jnp.bfloat16), input_grad, weight_grads[0], weight_grads[1], weight_grads[2], weight_grads[3], weight_grads[4], weight_grads[5], weight_grads[6], weight_grads[7], weight_grads[8], weight_grads[9], weight_grads[10], weight_grads[11])
```

```python
import functools

import jax
import jax.numpy as jnp
from jax import lax
from jax.experimental import pallas as pl
from jax.experimental.pallas import tpu as pltpu
from jax.sharding import PartitionSpec as P

HEAD = 64
PLANE = 8
LOG2E = 1.4426950408889634
BF = jnp.bfloat16
F32 = jnp.float32


def dot(left, right, dims):
    return lax.dot_general(left, right, ((dims[0], dims[1]), ((), ())), preferred_element_type=F32)


def attend_fwd_kernel(qt_ref, kt_ref, vt_ref, idq_ref, idk_ref, ct_ref, lse_ref):
    keys = kt_ref[...].T
    values_t = vt_ref[...]
    factor = HEAD**-0.5 * LOG2E
    tile = 256
    for start in range(0, qt_ref.shape[1], tile):
        cols = slice(start, start + tile)
        scores = dot(keys, qt_ref[:, cols], ((1,), (0,)))
        scores = jnp.where(idk_ref[...] == idq_ref[:, cols], scores, -1e30)
        top = jnp.max(scores, axis=0, keepdims=True)
        probs = jnp.exp2((scores - top) * factor)
        total = jnp.sum(probs, axis=0, keepdims=True)
        context = dot(values_t, probs.astype(BF), ((1,), (0,)))
        ct_ref[:, cols] = (context / total).astype(BF)
        lse_ref[0, :, cols] = top * factor + jnp.log2(total)


def attend_fwd(qt, kt, vt, idq, idk):
    width, queries = qt.shape
    keys = kt.shape[1]
    heads = width // HEAD
    return pl.pallas_call(
        attend_fwd_kernel,
        grid=(heads,),
        in_specs=[
            pl.BlockSpec((HEAD, queries), lambda h: (h, 0)),
            pl.BlockSpec((HEAD, keys), lambda h: (h, 0)),
            pl.BlockSpec((HEAD, keys), lambda h: (h, 0)),
            pl.BlockSpec((1, queries), lambda h: (0, 0)),
            pl.BlockSpec((keys, 1), lambda h: (0, 0)),
        ],
        out_specs=[
            pl.BlockSpec((HEAD, queries), lambda h: (h, 0)),
            pl.BlockSpec((1, 1, queries), lambda h: (h, 0, 0)),
        ],
        out_shape=[
            jax.ShapeDtypeStruct((width, queries), BF),
            jax.ShapeDtypeStruct((heads, 1, queries), F32),
        ],
        compiler_params=pltpu.CompilerParams(vmem_limit_bytes=40 * 2**20),
        cost_estimate=pl.CostEstimate(
            flops=16 * width * queries * keys,
            bytes_accessed=8 * width * keys,
            transcendentals=heads * queries * keys,
        ),
        name="attend_fwd",
    )(qt, kt, vt, idq, idk)


def attend_bwd_kernel(
    qt_ref, kt_ref, vt_ref, ct_ref, dct_ref, lse_ref, idq_ref, idk_ref, dqt_ref, dkt_ref, dvt_ref
):
    keys_t = kt_ref[...]
    keys = keys_t.T
    values = vt_ref[...].T
    scale = HEAD**-0.5
    tile = 256
    dkt = jnp.zeros(keys_t.shape, F32)
    dvt = jnp.zeros(keys_t.shape, F32)
    for start in range(0, qt_ref.shape[1], tile):
        cols = slice(start, start + tile)
        queries_t = qt_ref[:, cols]
        grad_t = dct_ref[:, cols]
        scores = dot(keys, queries_t, ((1,), (0,)))
        scores = jnp.where(idk_ref[...] == idq_ref[:, cols], scores, -1e30)
        probs = jnp.exp2(scores * (scale * LOG2E) - lse_ref[0, :, cols])
        along = jnp.sum(
            grad_t.astype(F32) * ct_ref[:, cols].astype(F32), axis=0, keepdims=True
        )
        probs_grad = dot(values, grad_t, ((1,), (0,)))
        scores_grad = (probs * (probs_grad - along)).astype(BF)
        dvt += dot(grad_t, probs.astype(BF), ((1,), (1,)))
        dkt += dot(queries_t, scores_grad, ((1,), (1,)))
        dqt_ref[:, cols] = (dot(keys_t, scores_grad, ((1,), (0,))) * scale).astype(BF)
    dkt_ref[...] = (dkt * scale).astype(BF)
    dvt_ref[...] = dvt.astype(BF)


def attend_bwd(qt, kt, vt, ct, dct, lse, idq, idk):
    width, queries = qt.shape
    keys = kt.shape[1]
    heads = width // HEAD
    by_queries = pl.BlockSpec((HEAD, queries), lambda h: (h, 0))
    by_keys = pl.BlockSpec((HEAD, keys), lambda h: (h, 0))
    return pl.pallas_call(
        attend_bwd_kernel,
        grid=(heads,),
        in_specs=[
            by_queries,
            by_keys,
            by_keys,
            by_queries,
            by_queries,
            pl.BlockSpec((1, 1, queries), lambda h: (h, 0, 0)),
            pl.BlockSpec((1, queries), lambda h: (0, 0)),
            pl.BlockSpec((keys, 1), lambda h: (0, 0)),
        ],
        out_specs=[by_queries, by_keys, by_keys],
        out_shape=[
            jax.ShapeDtypeStruct((width, queries), BF),
            jax.ShapeDtypeStruct((width, keys), BF),
            jax.ShapeDtypeStruct((width, keys), BF),
        ],
        compiler_params=pltpu.CompilerParams(vmem_limit_bytes=40 * 2**20),
        cost_estimate=pl.CostEstimate(
            flops=40 * width * queries * keys,
            bytes_accessed=16 * width * keys,
            transcendentals=heads * queries * keys,
        ),
        name="attend_bwd",
    )(qt, kt, vt, ct, dct, lse, idq, idk)


def layer_norm(inputs, scaling, offset):
    center = inputs - jnp.mean(inputs, axis=-1, keepdims=True)
    spread = jnp.mean(center * center, axis=-1, keepdims=True)
    return center * lax.rsqrt(spread + 1e-05) * scaling + offset


def exact_gelu(values):
    return jax.nn.gelu(values, approximate=False)


def product(form, left, right):
    return jnp.einsum(form, left, right, preferred_element_type=F32)


class Moves:
    def __init__(self, dp, lines):
        self.dp, self.lines = dp, lines
        self.t = lax.axis_index("tensor")
        self.d = lax.axis_index("dp")
        self.e = self.d % PLANE
        self.c = self.d % 2
        self.first = [(i, i ^ (2 if i % 2 == 0 else 4)) for i in range(dp)]
        self.second = [(i, i ^ (4 if i % 2 == 0 else 2)) for i in range(dp)]
        self.core = [(i, i ^ 1) for i in range(dp)]
        self.to_owner = ([], [])
        for i in range(dp):
            for z in range(lines):
                for which in range(2):
                    row = (z + which) % 2
                    target = (i - i % 2 + z // 2) * lines + 2 * (i % 2) + row
                    self.to_owner[which].append((i * lines + z, target))
        self.to_home = tuple([(b, a) for a, b in pairs] for pairs in self.to_owner)

    def flip(self, value, pairs):
        return lax.ppermute(value, "dp", pairs)

    def from_line(self, value, step):
        pairs = [((i + step) % self.lines, i) for i in range(self.lines)]
        return lax.ppermute(value, "tensor", pairs)

    def to_line(self, value, step):
        pairs = [(i, (i + step) % self.lines) for i in range(self.lines)]
        return lax.ppermute(value, "tensor", pairs)

    def rows_to_owner(self, blocks):
        even = self.t % 2 == 0
        sent = (
            jnp.where(even, blocks[0], blocks[1]),
            jnp.where(even, blocks[1], blocks[0]),
        )
        got = [lax.ppermute(sent[k], ("dp", "tensor"), self.to_owner[k]) for k in range(2)]
        return jnp.concatenate(got, axis=0)

    def rows_to_home(self, half):
        size = half.shape[0] // 2
        got = [
            lax.ppermute(half[k * size : (k + 1) * size], ("dp", "tensor"), self.to_home[k])
            for k in range(2)
        ]
        even = self.t % 2 == 0
        return jnp.stack([jnp.where(even, got[0], got[1]), jnp.where(even, got[1], got[0])])

    def plane_gather(self, piece):
        parts = [piece]
        parts += [self.flip(part, self.first) for part in parts]
        parts += [self.flip(part, self.second) for part in parts]
        parts += [self.flip(part, self.core) for part in parts]
        table = jnp.array([[0, 4, 1, 6, 2, 5, 3, 7], [0, 4, 2, 5, 1, 6, 3, 7]], jnp.int32)
        stacked = jnp.stack(parts)
        return jnp.stack(
            [
                lax.dynamic_index_in_dim(
                    stacked, table[self.c, self.e ^ place], axis=0, keepdims=False
                )
                for place in range(PLANE)
            ]
        )

    def shard_gather(self, shard):
        rows = shard.shape[0] // PLANE
        piece = lax.dynamic_slice_in_dim(shard, self.e * rows, rows, axis=0)
        pieces = jnp.stack([self.from_line(piece, s) for s in range(1, self.lines)])
        whole = self.plane_gather(pieces)
        whole = jnp.moveaxis(whole, 0, 1).reshape((self.lines - 1,) + shard.shape)
        return jnp.concatenate([shard[None], whole], axis=0)

    def shard_reduce(self, grads):
        lines, rows, width = grads.shape
        size = rows // PLANE
        parts = grads.reshape(lines, 4, 2, size, width)
        x_bit, y_bit = (self.e // 2) % 2, self.e // 4
        zero = self.c == 0

        def pick(values, index, axis):
            return lax.dynamic_index_in_dim(values, index, axis=axis, keepdims=False)

        def join(kept, got):
            return (kept.astype(F32) + got.astype(F32)).astype(BF)

        got = self.flip(pick(parts, 1 - self.c, 2), self.core)
        parts = join(pick(parts, self.c, 2), got)
        keep = [jnp.where(zero, 2 * k + x_bit, 2 * y_bit + k) for k in range(2)]
        send = [jnp.where(zero, 2 * k + 1 - x_bit, 2 * (1 - y_bit) + k) for k in range(2)]
        got = self.flip(jnp.stack([pick(parts, i, 1) for i in send], axis=1), self.first)
        parts = join(jnp.stack([pick(parts, i, 1) for i in keep], axis=1), got)
        mine = jnp.where(zero, y_bit, x_bit)
        got = self.flip(pick(parts, 1 - mine, 1), self.second)
        parts = join(pick(parts, mine, 1), got)
        total = parts[0].astype(F32)
        for s in range(1, lines):
            total = total + self.to_line(parts[s], s).astype(F32)
        if self.dp > PLANE:
            groups = [[i + PLANE * g for g in range(self.dp // PLANE)] for i in range(PLANE)]
            total = lax.psum(total, "dp", axis_index_groups=groups)
        whole = self.plane_gather(total.astype(BF))
        return whole.reshape(rows, width).astype(F32)


def body(
    dp,
    lines,
    tokens,
    segment_ids,
    gain_first,
    shift_first,
    weight_qkv,
    bias_qv,
    weight_out,
    bias_out,
    gain_second,
    shift_second,
    weight_up,
    bias_up,
    weight_down,
    bias_down,
    cotangent,
):
    moves = Moves(dp, lines)
    t, c = moves.t, moves.c
    block, width = tokens.shape[1:]
    part = weight_qkv.shape[2]
    hidden = weight_up.shape[1]
    half = 2 * block

    x_half = moves.rows_to_owner(tokens)
    qkv_all = moves.shard_gather(weight_qkv.reshape(width, 3 * part))
    low = jnp.concatenate([bias_qv.reshape(-1), bias_up])
    biases = jnp.stack([low] + [moves.from_line(low, s) for s in range(1, lines)])
    bias_q = biases[:, :part].reshape(width, 1)
    bias_v = biases[:, part : 2 * part].reshape(width, 1)
    bias_hidden = biases[:, None, 2 * part :]
    other_ids = moves.flip(segment_ids, moves.core)
    id_rows = jnp.where(c == t // 2, segment_ids, other_ids)
    id_row = lax.dynamic_index_in_dim(id_rows, t % 2, axis=0, keepdims=False).reshape(lines, block)

    def half_ids(core):
        first = lax.dynamic_index_in_dim(id_row, 2 * core + t % 2, axis=0, keepdims=False)
        second = lax.dynamic_index_in_dim(id_row, 2 * core + 1 - t % 2, axis=0, keepdims=False)
        return jnp.concatenate([first, second])

    ids_own = half_ids(c)
    idq = ids_own[None, :]
    idk = jnp.concatenate([ids_own, half_ids(1 - c)])[:, None]

    out_all = moves.shard_gather(weight_out)
    up_all = moves.shard_gather(weight_up)
    down_all = moves.shard_gather(weight_down)
    grad_half = moves.rows_to_owner(cotangent)

    inputs = x_half.astype(F32)
    normed = layer_norm(inputs, gain_first, shift_first).astype(BF)
    qkv_all = qkv_all.reshape(lines, width, 3, part)
    qkv_t = product("skjp,tk->jspt", qkv_all, normed).reshape(3, width, half)
    qt = (qkv_t[0] + bias_q).astype(BF)
    kv_own = jnp.stack([qkv_t[1], qkv_t[2] + bias_v]).astype(BF)
    kv_other = moves.flip(kv_own, moves.core)
    kt, vt = jnp.concatenate([kv_own, kv_other], axis=2)
    ct, lse = attend_fwd(qt, kt, vt, idq, idk)
    out_flat = out_all.reshape(width, width)
    middle = inputs + product("jt,jd->td", ct, out_flat) + bias_out
    normed_second = layer_norm(middle, gain_second, shift_second).astype(BF)
    hidden_pre = product("td,sdf->stf", normed_second, up_all) + bias_hidden
    active, gelu_pull = jax.vjp(exact_gelu, hidden_pre)
    active = active.astype(BF)
    fed_forward = product("stf,sfd->td", active, down_all)
    block_out = moves.rows_to_home((middle + fed_forward + bias_down).astype(BF))

    down_grad = moves.shard_reduce(product("stf,td->sfd", active, grad_half).astype(BF))
    active_grad = product("td,sfd->stf", grad_half, down_all)
    pre_grad = gelu_pull(active_grad)[0].astype(BF)
    up_grad = moves.shard_reduce(product("td,stf->sdf", normed_second, pre_grad).astype(BF))
    upbias_grad = jnp.sum(pre_grad.astype(F32), axis=1)
    normed_grad = product("stf,sdf->td", pre_grad, up_all)
    norm_pull = jax.vjp(layer_norm, middle, gain_second, shift_second)[1]
    middle_part, gain_two, shift_two = norm_pull(normed_grad)
    grad_float = grad_half.astype(F32)
    middle_grad = grad_float + middle_part

    middle_low = middle_grad.astype(BF)
    out_grad = product("jt,td->jd", ct, middle_low).astype(BF)
    out_grad = moves.shard_reduce(out_grad.reshape(lines, part, width))
    dct = product("jd,td->jt", out_flat, middle_low).astype(BF)
    dqt, dkt, dvt = attend_bwd(qt, kt, vt, ct, dct, lse, idq, idk)
    partial = jnp.stack([dkt, dvt])
    got = moves.flip(partial[:, :, half:], moves.core)
    dkv = (partial[:, :, :half].astype(F32) + got.astype(F32)).astype(BF)
    stacked = jnp.concatenate([dqt[None], dkv]).reshape(3, lines, part, half)
    qkv_grad = product("tk,jspt->skjp", normed, stacked).astype(BF)
    qkv_grad = moves.shard_reduce(qkv_grad.reshape(lines, width, 3 * part))
    normed_grad = product("jspt,skjp->tk", stacked, qkv_all)
    norm_pull = jax.vjp(layer_norm, inputs, gain_first, shift_first)[1]
    input_part, gain_one, shift_one = norm_pull(normed_grad)
    input_grad = moves.rows_to_home((middle_grad + input_part).astype(BF)).astype(F32)

    bias_sums = jnp.concatenate(
        [
            jnp.sum(dqt.astype(F32), axis=1).reshape(lines, part),
            jnp.sum(dkv[1].astype(F32), axis=1).reshape(lines, part),
            upbias_grad,
        ],
        axis=1,
    )
    sums = jnp.concatenate(
        [
            jnp.roll(bias_sums, t, axis=0).reshape(-1),
            gain_one,
            shift_one,
            jnp.sum(middle_grad, axis=0),
            gain_two,
            shift_two,
            jnp.sum(grad_float, axis=0),
        ]
    )
    sums = lax.psum(sums, ("dp", "tensor"))
    own = bias_sums.shape[1]
    mine = lax.dynamic_slice_in_dim(sums, t * own, own)
    totals = sums[lines * own :].reshape(6, width)
    return (
        block_out,
        input_grad,
        totals[0],
        totals[1],
        qkv_grad.reshape(width, 3, part),
        mine[: 2 * part].reshape(2, part),
        out_grad,
        totals[2],
        totals[3],
        totals[4],
        up_grad,
        mine[2 * part :],
        down_grad,
        totals[5],
    )


def solution(mesh):
    in_specs = (
        P("dp", "tensor", None),
        P("dp", None),
        P(),
        P(),
        P(None, None, "tensor"),
        P(None, "tensor"),
        P("tensor", None),
        P(),
        P(),
        P(),
        P(None, "tensor"),
        P("tensor"),
        P("tensor", None),
        P(),
        P("dp", "tensor", None),
    )
    out_specs = (
        P("dp", "tensor", None),
        P("dp", "tensor", None),
        P(),
        P(),
        P(None, None, "tensor"),
        P(None, "tensor"),
        P("tensor", None),
        P(),
        P(),
        P(),
        P(None, "tensor"),
        P("tensor"),
        P("tensor", None),
        P(),
    )
    whole = functools.partial(body, mesh.shape["dp"], mesh.shape["tensor"])
    return jax.shard_map(whole, mesh=mesh, in_specs=in_specs, out_specs=out_specs, check_vma=False)
```

```python
import functools

import jax
import jax.numpy as jnp
from jax import lax
from jax.experimental import pallas as pl
from jax.experimental.pallas import tpu as pltpu
from jax.sharding import PartitionSpec as P

HEAD = 64
PLANE = 8
FACTOR = HEAD**-0.5 * 1.4426950408889634
BF = jnp.bfloat16
F32 = jnp.float32
NN = ((1,), (0,))
NT = ((1,), (1,))
TN = ((0,), (0,))
ATT, UP, DOWN = 0, 1, 2


def dot(left, right, dims):
    return lax.dot_general(left, right, (dims, ((), ())), preferred_element_type=F32)


def norm_parts(values):
    center = values - jnp.mean(values, axis=-1, keepdims=True)
    rate = lax.rsqrt(jnp.mean(center * center, axis=-1, keepdims=True) + 1e-5)
    return center * rate, rate


def norm_back(normed, rate, grad, gain):
    scaled = grad * gain
    mean = jnp.mean(scaled, axis=-1, keepdims=True)
    along = jnp.mean(scaled * normed, axis=-1, keepdims=True)
    return rate * (scaled - mean - normed * along)


def column_sum(values):
    return jnp.sum(values, axis=0, keepdims=True)


def layer_kernel(
    lines,
    whole_plane,
    tokens,
    cotangent,
    ids_in,
    shard_att,
    shard_up,
    shard_down,
    bias_in,
    vectors,
    block_home,
    input_home,
    grads_out,
    small_out,
    w,
    r_core,
    r_a,
    r_b,
    r_z,
    xb,
    gb,
    ids,
    bias,
    mask,
    n1,
    n2,
    n2t,
    middle,
    acc,
    acc2,
    dmr,
    qt,
    kv,
    kvs,
    kvg,
    ct,
    lse,
    bo,
    ig,
    sums,
    sums_z,
    sums_p,
    s_loc,
    s_ids,
    s_bias,
    s_x,
    s_g,
    s_bo,
    s_ig,
    s_kv,
    s_kvg,
    s_z,
    s_1,
    s_2,
    s_3,
    s_c,
    s_a,
    s_b,
    s_zg,
    s_g1,
    s_g2,
    s_g3,
    s_sz,
    s_sp,
):
    t = lax.axis_index("tensor")
    d = lax.axis_index("dp")
    e = lax.rem(d, PLANE)
    base = d - e
    c = lax.rem(e, 2)
    yx = e // 2
    x_bit = lax.rem(yx, 2)
    y_bit = yx // 2
    half = 512
    part = 192

    yx_x = 2 * y_bit + 1 - x_bit
    yx_y = 2 * (1 - y_bit) + x_bit
    yx_xy = 2 * (1 - y_bit) + 1 - x_bit
    yx_first = (1 - c) * yx_x + c * yx_y
    yx_second = (1 - c) * yx_y + c * yx_x

    def at(dp_index, line):
        return {"dp": dp_index, "tensor": line}

    dev_core = at(base + 2 * yx + 1 - c, t)
    dev_first = at(base + 2 * yx_first + c, t)
    dev_second = at(base + 2 * yx_second + c, t)

    def offset(s):
        return s + (s // 2) * (1 - 2 * (s % 2))

    def line_before(s):
        return at(d, lax.rem(t - offset(s) + lines, lines))

    def line_after(s):
        return at(d, lax.rem(t + offset(s), lines))

    def remote(src, dst, sems, dev):
        return pltpu.make_async_remote_copy(
            src_ref=src,
            dst_ref=dst,
            send_sem=sems[0],
            recv_sem=sems[1],
            device_id=dev,
            device_id_type=pl.DeviceIdType.MESH,
        )

    def pair(sem, *index):
        return sem.at[(0,) + index], sem.at[(1,) + index]

    barrier = pltpu.get_barrier_semaphore()
    for step in range(lines):
        for core in range(2):
            if step == 0 and core == 0:
                continue
            other = base + 2 * yx + lax.rem(c + core, 2)
            pl.semaphore_signal(
                barrier,
                1,
                device_id=at(other, lax.rem(t + step, lines)),
                device_id_type=pl.DeviceIdType.MESH,
            )
    for dev in (dev_first, dev_second):
        pl.semaphore_signal(barrier, 1, device_id=dev, device_id_type=pl.DeviceIdType.MESH)
    pl.semaphore_wait(barrier, 2 * lines - 1 + 2)

    def to_owner(src, dst, sem):
        for m in range(2):
            here = jnp.logical_and(t == 2 * c + m, c == t // 2)
            place = lax.rem(t, 2)
            dev = at(base + 2 * yx + t // 2, 2 * c + m)

            @pl.when(here)
            def _():
                pltpu.make_async_copy(src.at[m], dst.at[place], sem.at[1, place]).start()

            @pl.when(jnp.logical_not(here))
            def _():
                remote(src.at[m], dst.at[place], (sem.at[0, m], sem.at[1, place]), dev).start()

    def to_owner_wait(src, dst, sem):
        for k in range(2):
            pltpu.make_async_copy(dst.at[k], dst.at[k], sem.at[1, k]).wait()

    def to_owner_sent(src, sem):
        for m in range(2):
            here = jnp.logical_and(t == 2 * c + m, c == t // 2)

            @pl.when(jnp.logical_not(here))
            def _():
                remote(src.at[m], src.at[m], (sem.at[0, m], sem.at[1, m]), dev_core).wait_send()

    def to_home(src, dst, sem):
        to_owner(src, dst, sem)

    shards = (shard_att, shard_up, shard_down)

    def gather_z(i, s):
        return remote(
            shards[i].at[yx, c], w.at[i, s, yx, c], pair(s_z, i, s - 1), line_before(s)
        )

    def gather_1(i, s):
        ref = w.at[i, s, yx, c]
        return remote(ref, ref, pair(s_1, i, s - 1), dev_first)

    def gather_2(i, s, k):
        ref = w.at[i, s, yx if k == 0 else yx_first, c]
        return remote(ref, ref, pair(s_2, i, s - 1, k), dev_second)

    def gather_3(i, s):
        ref = w.at[i, s, :, c]
        return remote(ref, ref, pair(s_3, i, s - 1), dev_core)

    def step_1(i, s):
        gather_z(i, s).wait_recv()
        gather_1(i, s).start()

    def step_2(i, s):
        gather_1(i, s).wait_recv()
        gather_2(i, s, 0).start()
        gather_2(i, s, 1).start()

    def step_3(i, s):
        gather_2(i, s, 0).wait_recv()
        gather_2(i, s, 1).wait_recv()
        gather_3(i, s).start()

    def step_4(i, s):
        gather_3(i, s).wait()
        gather_1(i, s).wait_send()
        gather_2(i, s, 0).wait_send()
        gather_2(i, s, 1).wait_send()

    def add_into(dst, src):
        dst[...] = (dst[...].astype(F32) + src[...].astype(F32)).astype(BF)

    keep_other = yx_second
    send_k = [(1 - c) * (2 * k + 1 - x_bit) + c * (2 * (1 - y_bit) + k) for k in range(2)]
    keep_k = [(1 - c) * (2 * k + x_bit) + c * (2 * y_bit + k) for k in range(2)]
    k_mine = (1 - c) * y_bit + c * x_bit

    def reduce_core(i, s):
        return remote(w.at[i, s, :, 1 - c], r_core.at[i, s], pair(s_c, i, s), dev_core)

    def reduce_a(i, s, k):
        return remote(w.at[i, s, send_k[k], c], r_a.at[i, s, k], pair(s_a, i, s, k), dev_first)

    def reduce_b(i, s):
        return remote(w.at[i, s, keep_other, c], r_b.at[i, s], pair(s_b, i, s), dev_second)

    def reduce_z(i, s):
        return remote(w.at[i, s, yx, c], r_z.at[i, s - 1], pair(s_zg, i, s - 1), line_after(s))

    def fold_1(i, s):
        reduce_core(i, s).start()

    def fold_2(i, s):
        reduce_core(i, s).wait_recv()
        for k in range(2):
            add_into(w.at[i, s, send_k[k], c], r_core.at[i, s, send_k[k]])
            reduce_a(i, s, k).start()
        for k in range(2):
            add_into(w.at[i, s, keep_k[k], c], r_core.at[i, s, keep_k[k]])

    def fold_3(i, s):
        reduce_a(i, s, 0).wait_recv()
        reduce_a(i, s, 1).wait_recv()
        add_into(w.at[i, s, keep_other, c], r_a.at[i, s, 1 - k_mine])
        reduce_b(i, s).start()
        add_into(w.at[i, s, yx, c], r_a.at[i, s, k_mine])

    def fold_4(i, s):
        reduce_b(i, s).wait_recv()
        add_into(w.at[i, s, yx, c], r_b.at[i, s])
        if isinstance(s, int):
            if s > 0:
                reduce_z(i, s).start()
        else:

            @pl.when(s > 0)
            def _():
                reduce_z(i, s).start()

    def spread_1(i):
        ref = grads_out.at[i, yx, c]
        return remote(ref, ref, pair(s_g1, i), dev_first)

    def spread_2(i, k):
        ref = grads_out.at[i, yx if k == 0 else yx_first, c]
        return remote(ref, ref, pair(s_g2, i, k), dev_second)

    def spread_3(i):
        ref = grads_out.at[i, :, c]
        return remote(ref, ref, pair(s_g3, i), dev_core)

    def total(i):
        out = w[i, 0, yx, c].astype(F32)
        for s in range(1, lines):
            reduce_z(i, s).wait_recv()
            out = out + r_z[i, s - 1].astype(F32)
        if whole_plane:
            w[i, 0, yx, c] = out.astype(BF)
            copy = pltpu.make_async_copy(w.at[i, 0, yx, c], grads_out.at[i, yx, c], s_loc.at[3 + i])
        else:
            acc[pl.ds(96 * i, 96), :] = out
            copy = pltpu.make_async_copy(
                acc.at[pl.ds(96 * i, 96)], grads_out.at[i], s_loc.at[3 + i]
            )
        copy.start()
        copy.wait()
        if whole_plane:
            spread_1(i).start()

    def spread_step_2(i):
        if whole_plane:
            spread_1(i).wait_recv()
            spread_2(i, 0).start()
            spread_2(i, 1).start()

    def spread_step_3(i):
        if whole_plane:
            spread_2(i, 0).wait_recv()
            spread_2(i, 1).wait_recv()
            spread_3(i).start()

    ids_copy = remote(ids_in, ids.at[c], pair(s_ids), dev_core)
    ids_copy.start()
    bias_copies = [
        remote(bias_in, bias.at[s], pair(s_bias, s - 1), line_before(s)) for s in range(1, lines)
    ]
    for copy in bias_copies:
        copy.start()
    for s in range(1, lines):
        gather_z(ATT, s).start()
    to_owner(tokens, xb, s_x)
    own = [pltpu.make_async_copy(shards[i], w.at[i, 0], s_loc.at[i]) for i in range(3)]
    for copy in own:
        copy.start()
    bias[0] = bias_in[...]
    ids[pl.ds(c, 1)] = ids_in[...][None]

    remote(ids_in, ids.at[1 - c], pair(s_ids), dev_core).wait_recv()
    row = ids[t // 2, pl.ds(lax.rem(t, 2), 1), :].astype(F32)
    low, high = row[:, :half], row[:, half:]
    first_core = c == 0
    ids_own = jnp.where(first_core, low, high)
    ids_other = jnp.where(first_core, high, low)
    for place, ids_k in enumerate((ids_own, ids_other)):
        columns = jnp.broadcast_to(ids_k, (128, half)).T
        for j in range(0, half, 128):
            mask[place, :, j : j + 128] = jnp.where(columns == ids_own[:, j : j + 128], 0.0, -1e30)

    for s in range(1, lines):
        step_1(ATT, s)
    for s in range(1, lines):
        step_2(ATT, s)

    to_owner_wait(tokens, xb, s_x)
    for s in (1, 2):
        for i in (UP, DOWN):
            gather_z(i, s).start()
    normed, _ = norm_parts(xb[...].reshape(half, 768).astype(F32))
    n1[...] = (normed * vectors[0:1] + vectors[1:2]).astype(BF)
    for copy in bias_copies:
        copy.wait_recv()
    own[0].wait()

    def weights(i, s):
        return w[i, s].reshape(768, 768)

    def kv_copy(s):
        return remote(kv.at[s], kvs.at[s], pair(s_kv, s), dev_core)

    def project(s):
        qkv = dot(weights(ATT, s)[: 3 * part], n1[...], NT)
        bias_row = bias[s, 1:2, : 2 * part]
        bias_col = jnp.broadcast_to(bias_row, (128, 2 * part)).T[:, :1]
        qt[s] = (qkv[:part] + bias_col[:part]).astype(BF)
        kv[s, 0] = qkv[part : 2 * part].astype(BF)
        kv[s, 1] = (qkv[2 * part :] + bias_col[part:]).astype(BF)
        kv_copy(s).start()

    project(0)
    for s in range(1, lines):
        step_3(ATT, s)

    def attend(s, carry):
        @pl.when(s < lines - 1)
        def _():
            step_4(ATT, s + 1)
            project(s + 1)

        kv_copy(s).wait_recv()
        for h in range(part // HEAD):
            rows = slice(h * HEAD, (h + 1) * HEAD)
            q = qt[s, rows, :]
            s0 = dot(kv[s, 0, rows, :].T, q, NN) * FACTOR + mask[0]
            s1 = dot(kvs[s, 0, rows, :].T, q, NN) * FACTOR + mask[1]
            top = jnp.maximum(
                jnp.max(s0, axis=0, keepdims=True), jnp.max(s1, axis=0, keepdims=True)
            )
            p0 = jnp.exp2(s0 - top)
            p1 = jnp.exp2(s1 - top)
            weight = column_sum(p0) + column_sum(p1)
            out = dot(kv[s, 1, rows, :], p0.astype(BF), NN)
            out = out + dot(kvs[s, 1, rows, :], p1.astype(BF), NN)
            ct[s, rows, :] = (out / weight).astype(BF)
            lse[s, h : h + 1, :] = top + jnp.log2(weight)

        @pl.when(s == 0)
        def _():
            to_owner(cotangent, gb, s_g)

        @pl.when(s == 1)
        def _():
            step_1(UP, 1)
            step_1(DOWN, 1)

        @pl.when(s == 2)
        def _():
            step_2(UP, 1)
            step_2(DOWN, 1)
            step_1(UP, 2)
            step_1(DOWN, 2)
            gather_z(UP, 3).start()
            gather_z(DOWN, 3).start()

        @pl.when(s == 3)
        def _():
            step_3(UP, 1)
            step_3(DOWN, 1)
            step_2(UP, 2)
            step_2(DOWN, 2)

        return carry

    lax.fori_loop(0, lines, attend, 0)

    mid = xb[...].reshape(half, 768).astype(F32) + vectors[2:3]
    for s in range(lines):
        mid = mid + dot(ct[s], weights(ATT, s)[3 * part :], TN)
    middle[...] = mid
    normed, _ = norm_parts(mid)
    low_normed = (normed * vectors[3:4] + vectors[4:5]).astype(BF)
    n2[...] = low_normed
    n2t[...] = low_normed.T
    acc[...] = jnp.zeros_like(acc)
    acc2[...] = jnp.zeros_like(acc2)
    own[1].wait()
    own[2].wait()
    to_owner_wait(cotangent, gb, s_g)

    def feed(s, carry):
        @pl.when(s > 0)
        def _():
            step_4(UP, s)
            step_4(DOWN, s)

        grad = gb[...].reshape(half, 768)
        pre = dot(n2[...], weights(UP, s), NN) + bias[s, 0:1, :]
        phi = 0.5 * (1.0 + lax.erf(pre * 0.7071067811865476))
        active = (pre * phi).astype(BF)
        slope = phi + pre * jnp.exp(-0.5 * pre * pre) * 0.3989422804014327
        acc[...] += dot(active, weights(DOWN, s), NN)
        pre_grad = (dot(grad, weights(DOWN, s), NT) * slope).astype(BF)
        sums[s, 0:1, :] = column_sum(pre_grad.astype(F32))
        acc2[...] += dot(pre_grad, weights(UP, s), NT)
        w[DOWN, s] = dot(active, grad, TN).astype(BF).reshape(4, 2, 96, 768)
        fold_1(DOWN, s)
        w[UP, s] = dot(n2t[...], pre_grad, NN).astype(BF).reshape(4, 2, 96, 768)
        fold_1(UP, s)

        @pl.when(s == 0)
        def _():
            step_3(UP, 2)
            step_3(DOWN, 2)
            step_1(UP, 3)
            step_1(DOWN, 3)

        @pl.when(s == 1)
        def _():
            step_2(UP, 3)
            step_2(DOWN, 3)

        @pl.when(s == 2)
        def _():
            step_3(UP, 3)
            step_3(DOWN, 3)

        @pl.when(s >= 1)
        def _():
            fold_2(DOWN, s - 1)
            fold_2(UP, s - 1)

        @pl.when(s >= 2)
        def _():
            fold_3(DOWN, s - 2)
            fold_3(UP, s - 2)

        @pl.when(s >= 3)
        def _():
            fold_4(DOWN, s - 3)
            fold_4(UP, s - 3)

        return carry

    lax.fori_loop(0, lines, feed, 0)

    mid = middle[...]
    bo[...] = (mid + acc[...] + vectors[5:6]).astype(BF).reshape(2, 256, 768)
    to_home(bo, block_home, s_bo)
    normed, rate = norm_parts(mid)
    grad = gb[...].reshape(half, 768).astype(F32)
    back = acc2[...]
    middle_grad = grad + norm_back(normed, rate, back, vectors[3:4])
    vec_out = column_sum(middle_grad)
    vec_gain = column_sum(back * normed)
    vec_shift = column_sum(back)
    vec_down = column_sum(grad)
    for s in range(lines):
        sums[s, 4:5, :] = vec_out
        sums[s, 5:6, :] = vec_gain
        sums[s, 6:7, :] = vec_shift
        sums[s, 7:8, :] = vec_down
    acc2[...] = middle_grad
    dmr[...] = middle_grad.astype(BF)
    acc[...] = jnp.zeros_like(acc)

    def kvg_copy(s):
        return remote(kvs.at[s], kvg.at[s], pair(s_kvg, s), dev_core)

    def finish(s):
        kvg_copy(s).wait_recv()
        dq = qt[s]
        dkv = (kv[s].astype(F32) + kvg[s].astype(F32)).astype(BF).reshape(2 * part, half)
        ones = jnp.ones((8, half), BF)
        sums[s, 1:2, :part] = dot(ones, dq, NT)[:1]
        sums[s, 1:2, part : 2 * part] = dot(ones, dkv[part:], NT)[:1]
        sums[s, 1:2, 2 * part :] = jnp.zeros((1, 768 - 2 * part), F32)
        stacked = jnp.concatenate([dq, dkv], axis=0)
        acc[...] += dot(stacked, weights(ATT, s)[: 3 * part], TN)
        w[ATT, s, 0:3] = dot(stacked, n1[...], NN).astype(BF).reshape(3, 2, 96, 768)
        fold_1(ATT, s)

    def attend_back(s, carry):
        dct = dot(w[ATT, s, 3].reshape(part, 768), dmr[...], NT).astype(BF)
        w[ATT, s, 3] = dot(ct[s], dmr[...], NN).astype(BF).reshape(2, 96, 768)
        kv_copy(s).wait_send()
        for h in range(part // HEAD):
            rows = slice(h * HEAD, (h + 1) * HEAD)
            g = dct[rows]
            q = qt[s, rows, :]
            along = column_sum(g.astype(F32) * ct[s, rows, :].astype(F32))
            total_log = lse[s, h : h + 1, :]
            dq = jnp.zeros((HEAD, half), F32)
            for place, ref in enumerate((kv, kvs)):
                k = ref[s, 0, rows, :]
                v = ref[s, 1, rows, :]
                p = jnp.exp2(dot(k.T, q, NN) * FACTOR + mask[place] - total_log)
                ds = (p * (dot(v.T, g, NN) - along)).astype(BF)
                ref[s, 0, rows, :] = (dot(q, ds, NT) * HEAD**-0.5).astype(BF)
                ref[s, 1, rows, :] = dot(g, p.astype(BF), NT).astype(BF)
                dq = dq + dot(k, ds, NN)
            qt[s, rows, :] = (dq * HEAD**-0.5).astype(BF)
        kvg_copy(s).start()

        @pl.when(s == 0)
        def _():
            for i in (DOWN, UP):
                fold_2(i, 3)
                fold_3(i, 2)
                fold_4(i, 1)

        @pl.when(s == 1)
        def _():
            for i in (DOWN, UP):
                fold_3(i, 3)
                fold_4(i, 2)

        @pl.when(s == 2)
        def _():
            for i in (DOWN, UP):
                fold_4(i, 3)
            fold_2(ATT, 0)

        @pl.when(s == 3)
        def _():
            total(DOWN)
            total(UP)
            fold_2(ATT, 1)
            fold_3(ATT, 0)

        @pl.when(s > 0)
        def _():
            finish(s - 1)

        return carry

    lax.fori_loop(0, lines, attend_back, 0)
    finish(3)

    normed, rate = norm_parts(xb[...].reshape(half, 768).astype(F32))
    back = acc[...]
    ig[...] = (
        (acc2[...] + norm_back(normed, rate, back, vectors[0:1])).astype(BF).reshape(2, 256, 768)
    )
    to_home(ig, input_home, s_ig)
    vec_gain = column_sum(back * normed)
    vec_shift = column_sum(back)
    for s in range(lines):
        sums[s, 2:3, :] = vec_gain
        sums[s, 3:4, :] = vec_shift

    def sums_copy(s):
        return remote(sums.at[s], sums_z.at[t], pair(s_sz, s - 1), line_after(s))

    for s in range(1, lines):
        sums_copy(s).start()
    sums_z[pl.ds(t, 1)] = sums[0:1]

    fold_2(ATT, 2)
    fold_3(ATT, 1)
    fold_4(ATT, 0)
    spread_step_2(DOWN)
    spread_step_2(UP)
    fold_2(ATT, 3)
    fold_3(ATT, 2)
    fold_4(ATT, 1)
    for s in range(1, lines):
        sums_copy(s).wait()
    sums_p[0] = (sums_z[0] + sums_z[1]) + (sums_z[2] + sums_z[3])

    dev_x = at(base + 2 * yx_x + c, t)
    dev_y = at(base + 2 * yx_y + c, t)

    def flip(k):
        return remote(
            sums_p.at[2 * k], sums_p.at[2 * k + 1], pair(s_sp, k), (dev_core, dev_x, dev_y)[k]
        )

    flip(0).start()
    spread_step_3(DOWN)
    spread_step_3(UP)
    fold_3(ATT, 3)
    fold_4(ATT, 2)
    flip(0).wait()
    sums_p[2] = sums_p[0] + sums_p[1]
    flip(1).start()
    fold_4(ATT, 3)
    flip(1).wait()
    sums_p[4] = sums_p[2] + sums_p[3]
    flip(2).start()
    total(ATT)
    flip(2).wait()
    small_out[...] = sums_p[4] + sums_p[5]
    spread_step_2(ATT)
    spread_step_3(ATT)

    ids_copy.wait_send()
    for copy in bias_copies:
        copy.wait_send()
    to_owner_sent(tokens, s_x)
    to_owner_sent(cotangent, s_g)
    to_owner_wait(bo, block_home, s_bo)
    to_owner_sent(bo, s_bo)
    to_owner_wait(ig, input_home, s_ig)
    to_owner_sent(ig, s_ig)
    for i in range(3):
        for s in range(1, lines):
            gather_z(i, s).wait_send()
            reduce_z(i, s).wait_send()
        for s in range(lines):
            reduce_core(i, s).wait_send()
            reduce_a(i, s, 0).wait_send()
            reduce_a(i, s, 1).wait_send()
            reduce_b(i, s).wait_send()
        if whole_plane:
            spread_1(i).wait_send()
            spread_2(i, 0).wait_send()
            spread_2(i, 1).wait_send()
            spread_3(i).wait()
    for s in range(lines):
        kvg_copy(s).wait_send()


def layer(lines, whole_plane, operands):
    def dma(*shape):
        return pltpu.SemaphoreType.DMA((2,) + shape)

    def vmem(*shape, dtype=BF):
        return pltpu.VMEM(shape, dtype)

    n = lines
    anywhere = pl.BlockSpec(memory_space=pl.ANY)
    inside = pl.BlockSpec(memory_space=pltpu.VMEM)
    piece = (96, 768)
    if whole_plane:
        grads = jax.ShapeDtypeStruct((3, 4, 2) + piece, BF)
    else:
        grads = jax.ShapeDtypeStruct((3,) + piece, F32)
    blocks = jax.ShapeDtypeStruct((2, 256, 768), BF)
    return pl.pallas_call(
        functools.partial(layer_kernel, lines, whole_plane),
        in_specs=[anywhere, anywhere, inside, anywhere, anywhere, anywhere, inside, inside],
        out_specs=[anywhere, anywhere, anywhere, inside],
        out_shape=[blocks, blocks, grads, jax.ShapeDtypeStruct((8, 768), F32)],
        scratch_shapes=[
            vmem(3, n, 4, 2, *piece),
            vmem(3, n, 4, *piece),
            vmem(3, n, 2, *piece),
            vmem(3, n, *piece),
            vmem(3, n - 1, *piece),
            vmem(2, 256, 768),
            vmem(2, 256, 768),
            vmem(2, 2, 1024, dtype=jnp.int32),
            vmem(n, 8, 768, dtype=F32),
            vmem(2, 512, 512, dtype=F32),
            vmem(512, 768),
            vmem(512, 768),
            vmem(768, 512),
            vmem(512, 768, dtype=F32),
            vmem(512, 768, dtype=F32),
            vmem(512, 768, dtype=F32),
            vmem(512, 768),
            vmem(n, 192, 512),
            vmem(n, 2, 192, 512),
            vmem(n, 2, 192, 512),
            vmem(n, 2, 192, 512),
            vmem(n, 192, 512),
            vmem(n, 8, 512, dtype=F32),
            vmem(2, 256, 768),
            vmem(2, 256, 768),
            vmem(n, 8, 768, dtype=F32),
            vmem(n, 8, 768, dtype=F32),
            vmem(6, 8, 768, dtype=F32),
            pltpu.SemaphoreType.DMA((6,)),
            dma(),
            dma(n - 1),
            dma(2),
            dma(2),
            dma(2),
            dma(2),
            dma(n),
            dma(n),
            dma(3, n - 1),
            dma(3, n - 1),
            dma(3, n - 1, 2),
            dma(3, n - 1),
            dma(3, n),
            dma(3, n, 2),
            dma(3, n),
            dma(3, n - 1),
            dma(3),
            dma(3, 2),
            dma(3),
            dma(n - 1),
            dma(3),
        ],
        compiler_params=pltpu.CompilerParams(
            collective_id=0, has_side_effects=True, vmem_limit_bytes=62 * 2**20
        ),
        name="layer",
    )(*operands)


def body(
    dp,
    lines,
    tokens,
    segment_ids,
    gain_first,
    shift_first,
    weight_qkv,
    bias_qv,
    weight_out,
    bias_out,
    gain_second,
    shift_second,
    weight_up,
    bias_up,
    weight_down,
    bias_down,
    cotangent,
):
    width = tokens.shape[2]
    part = weight_qkv.shape[2]
    shard = (4, 2, width // PLANE, width)
    att = jnp.concatenate([weight_qkv.reshape(width, 3 * part).T, weight_out], axis=0)
    low = jnp.concatenate([bias_qv.reshape(-1), jnp.zeros((width - 2 * part,), F32)])
    bias = jnp.concatenate([bias_up[None], low[None], jnp.zeros((6, width), F32)])
    zero = jnp.zeros((width,), F32)
    vectors = jnp.stack(
        [gain_first, shift_first, bias_out, gain_second, shift_second, bias_down, zero, zero]
    )
    whole_plane = dp == PLANE
    block_out, input_grad, grads, small = layer(
        lines,
        whole_plane,
        (
            tokens,
            cotangent,
            segment_ids,
            att.reshape(shard),
            weight_up.reshape(shard),
            weight_down.reshape(shard),
            bias,
            vectors,
        ),
    )
    if not whole_plane:
        apart = [[i + PLANE * g for g in range(dp // PLANE)] for i in range(PLANE)]
        planes = [[i + PLANE * g for i in range(PLANE)] for g in range(dp // PLANE)]
        grads, small = lax.psum((grads, small), "dp", axis_index_groups=apart)
        grads = lax.all_gather(grads.astype(BF), "dp", axis=1, axis_index_groups=planes)
    grads = grads.reshape(3, width, width).astype(F32)
    att_grad = grads[0]
    return (
        block_out,
        input_grad.astype(F32),
        small[2],
        small[3],
        att_grad[: 3 * part].T.reshape(width, 3, part),
        small[1, : 2 * part].reshape(2, part),
        att_grad[3 * part :],
        small[4],
        small[5],
        small[6],
        grads[1],
        small[0],
        grads[2],
        small[7],
    )


def solution(mesh):
    in_specs = (
        P("dp", "tensor", None),
        P("dp", None),
        P(),
        P(),
        P(None, None, "tensor"),
        P(None, "tensor"),
        P("tensor", None),
        P(),
        P(),
        P(),
        P(None, "tensor"),
        P("tensor"),
        P("tensor", None),
        P(),
        P("dp", "tensor", None),
    )
    out_specs = (
        P("dp", "tensor", None),
        P("dp", "tensor", None),
        P(),
        P(),
        P(None, None, "tensor"),
        P(None, "tensor"),
        P("tensor", None),
        P(),
        P(),
        P(),
        P(None, "tensor"),
        P("tensor"),
        P("tensor", None),
        P(),
    )
    whole = functools.partial(body, mesh.shape["dp"], mesh.shape["tensor"])
    return jax.shard_map(whole, mesh=mesh, in_specs=in_specs, out_specs=out_specs, check_vma=False)
```

```python
import functools

import jax
import jax.numpy as jnp
from jax import lax
from jax.experimental import pallas as pl
from jax.experimental.pallas import tpu as pltpu
from jax.sharding import PartitionSpec as P

HEAD = 64
PLANE = 8
FACTOR = HEAD**-0.5 * 1.4426950408889634
BF = jnp.bfloat16
F32 = jnp.float32
NN = ((1,), (0,))
NT = ((1,), (1,))
TN = ((0,), (0,))
ATT, FFN = 0, 1

Z_OWN, Z_PASS, STEP_1, STEP_2, STEP_3, FOLD_2, FOLD_3, FOLD_4, FOLD_5, TOTAL = range(10)
SPREAD_2, SPREAD_3, FINISH, SEE, SUMS, SUMS_Z, SUMS_P, SUMS_END, MOVE = range(10, 19)
X, G, BO, IG = range(4)
START, X_HERE, FIRST, ATTEND, OUT, FEED, BLOCK, NORM, BACK, TAIL_0, TAIL_1, TAIL_2, TAIL_3 = range(13)

ORDER = (3, 2, 1, 0)

PLAN = {
    (START,): (
        (Z_OWN, ATT),
        (Z_OWN, FFN),
        (Z_PASS, ATT, 1),
        (MOVE, X, 0, 0),
        (Z_PASS, FFN, 1),
        (STEP_1, ATT, 1),
        (MOVE, X, 1, 1),
        (Z_PASS, ATT, 2),
        (STEP_1, FFN, 1),
        (MOVE, X, 0, 1),
        (STEP_2, ATT, 1),
        (STEP_1, ATT, 2),
        (SEE,),
        (Z_PASS, FFN, 2),
        (MOVE, X, 1, 0),
        (STEP_2, ATT, 2),
        (STEP_2, FFN, 1),
        (Z_PASS, ATT, 3),
    ),
    (X_HERE,): (
        (MOVE, G, 0, 1),
        (STEP_3, ATT, 1),
        (STEP_1, ATT, 3),
    ),
    (FIRST,): (
        (STEP_1, FFN, 2),
    ),
    (ATTEND, 0, 0): (
        (STEP_3, ATT, 2),
    ),
    (ATTEND, 0, 1): (
        (STEP_2, ATT, 3),
    ),
    (ATTEND, 0, 2): (
        (Z_PASS, FFN, 3),
        (MOVE, G, 0, 0),
        (MOVE, G, 1, 0),
    ),
    (ATTEND, 1, 1): (
        (STEP_2, FFN, 2),
        (MOVE, G, 1, 1),
    ),
    (ATTEND, 1, 2): (
        (STEP_3, ATT, 3),
    ),
    (ATTEND, 2, 0): (
        (STEP_3, FFN, 1),
    ),
    (ATTEND, 3, 0): (
        (STEP_1, FFN, 3),
    ),
    (OUT,): (
        (STEP_3, FFN, 2),
    ),
    (FEED, 0, 2): (
        (STEP_2, FFN, 3),
    ),
    (FEED, 1, 5): (
        (FOLD_2, FFN, 0),
        (STEP_3, FFN, 3),
    ),
    (FEED, 2, 5): (
        (FOLD_2, FFN, 1),
    ),
    (BLOCK,): (
        (MOVE, BO, 0, 0),
        (MOVE, BO, 1, 1),
    ),
    (NORM,): (
        (MOVE, BO, 1, 0),
    ),
    (BACK, 0, 0): (
        (FOLD_2, FFN, 2),
    ),
    (BACK, 1, 0): (
        (FOLD_2, FFN, 3),
        (FINISH, 3),
    ),
    (BACK, 1, 2): (
        (FOLD_2, ATT, 3),
    ),
    (BACK, 1, 3): (
        (MOVE, BO, 0, 1),
        (FOLD_3, FFN, 3),
        (FOLD_3, FFN, 2),
        (FINISH, 2),
    ),
    (BACK, 2, 0): (
        (FOLD_4, FFN, 3),
        (FOLD_3, ATT, 3),
    ),
    (BACK, 2, 3): (
        (FOLD_2, ATT, 2),
        (FOLD_4, ATT, 3),
        (FOLD_3, FFN, 1),
    ),
    (BACK, 3, 0): (
        (FOLD_5, FFN, 3),
        (FOLD_4, FFN, 2),
        (FOLD_3, FFN, 0),
    ),
    (BACK, 3, 1): (
        (FINISH, 1),
        (FOLD_5, ATT, 3),
    ),
    (BACK, 3, 2): (
        (FOLD_3, ATT, 2),
    ),
    (BACK, 3, 3): (
        (FOLD_4, FFN, 1),
        (FOLD_5, FFN, 1),
        (FOLD_2, ATT, 1),
    ),
    (TAIL_0,): (
        (FOLD_5, FFN, 2),
        (FINISH, 0),
        (FOLD_4, FFN, 0),
    ),
    (TAIL_2,): (
        (SUMS,),
        (FOLD_4, ATT, 2),
        (MOVE, IG, 1, 1),
        (FOLD_3, ATT, 1),
        (FOLD_2, ATT, 0),
        (TOTAL, FFN),
    ),
    (TAIL_3,): (
        (FOLD_4, ATT, 1),
        (FOLD_5, ATT, 2),
        (MOVE, IG, 0, 1),
        (FOLD_5, ATT, 1),
        (SUMS_Z,),
        (MOVE, IG, 0, 0),
        (FOLD_3, ATT, 0),
        (MOVE, IG, 1, 0),
        (SPREAD_2, FFN),
        (SUMS_P, 1),
        (FOLD_4, ATT, 0),
        (TOTAL, ATT),
        (SPREAD_2, ATT),
        (SPREAD_3, FFN),
        (SPREAD_3, ATT),
        (SUMS_P, 2),
        (SUMS_END,),
    ),
}


def dot(left, right, dims):
    return lax.dot_general(left, right, (dims, ((), ())), preferred_element_type=F32)


def norm_parts(values):
    center = values - jnp.mean(values, axis=-1, keepdims=True)
    rate = lax.rsqrt(jnp.mean(center * center, axis=-1, keepdims=True) + 1e-5)
    return center * rate, rate


def norm_back(normed, rate, grad, gain):
    scaled = grad * gain
    mean = jnp.mean(scaled, axis=-1, keepdims=True)
    along = jnp.mean(scaled * normed, axis=-1, keepdims=True)
    return rate * (scaled - mean - normed * along)


def column_sum(values):
    return jnp.sum(values, axis=0, keepdims=True)


def layer_kernel(
    lines,
    whole_plane,
    tokens,
    cotangent,
    ids_in,
    shard_qkv,
    shard_out,
    shard_up,
    shard_down,
    bias_up,
    bias_qv,
    gain_first,
    shift_first,
    bias_out,
    gain_second,
    shift_second,
    bias_down,
    block_home,
    input_home,
    grads_att,
    grads_up,
    grads_down,
    small_out,
    w_att,
    w_ffn,
    r_core_att,
    r_core_ffn,
    r_a_att,
    r_a_ffn,
    r_b_att,
    r_b_ffn,
    r_z_att,
    r_z_ffn,
    xb,
    gb,
    ids,
    bias,
    mask,
    n1,
    n2,
    n2t,
    middle,
    acc,
    acc2,
    dmr,
    qt,
    kv,
    kvs,
    kvg,
    ct,
    lse,
    bo,
    ig,
    sums,
    sums_z,
    sums_p,
    s_loc,
    s_ids,
    s_bias,
    s_x,
    s_g,
    s_bo,
    s_ig,
    s_kv,
    s_kvg,
    s_zs,
    s_zr,
    s_1,
    s_2,
    s_3,
    s_c,
    s_a,
    s_b,
    s_zgs,
    s_zgr,
    s_g1,
    s_g2,
    s_g3,
    s_sz,
    s_sp,
):
    t = lax.axis_index("tensor")
    d = lax.axis_index("dp")
    e = lax.rem(d, PLANE)
    base = d - e
    c = lax.rem(e, 2)
    yx = e // 2
    x_bit = lax.rem(yx, 2)
    y_bit = yx // 2
    half = 512
    part = 192
    width = 768
    w_of = (w_att, w_ffn)
    r_core = (r_core_att, r_core_ffn)
    r_a = (r_a_att, r_a_ffn)
    r_b = (r_b_att, r_b_ffn)
    r_z = (r_z_att, r_z_ffn)
    grads_out = ((grads_att,), (grads_up, grads_down))
    gain_first, shift_first, bias_out = [r[...][None] for r in (gain_first, shift_first, bias_out)]
    gain_second, shift_second = gain_second[...][None], shift_second[...][None]
    bias_down = bias_down[...][None]

    yx_x = 2 * y_bit + 1 - x_bit
    yx_y = 2 * (1 - y_bit) + x_bit
    yx_first = (1 - c) * yx_x + c * yx_y
    yx_second = (1 - c) * yx_y + c * yx_x

    def at(dp_index, line):
        return {"dp": dp_index, "tensor": line}

    dev_core = at(base + 2 * yx + 1 - c, t)
    dev_first = at(base + 2 * yx_first + c, t)
    dev_second = at(base + 2 * yx_second + c, t)

    def by_line_of(place, *values):
        out = values[3]
        for k in (2, 1, 0):
            out = jnp.where(place == k, values[k], out)
        return out

    def by_line(*values):
        return by_line_of(t, *values)

    source = [t, by_line(1, 2, 3, 2), by_line(2, 0, 1, 1), by_line(3, 3, 0, 0)]
    inner = jnp.logical_and(t > 0, t < lines - 1)
    outer = jnp.logical_not(inner)

    def remote(src, dst, sems, dev):
        return pltpu.make_async_remote_copy(
            src_ref=src,
            dst_ref=dst,
            send_sem=sems[0],
            recv_sem=sems[1],
            device_id=dev,
            device_id_type=pl.DeviceIdType.MESH,
        )

    def pair(sem, *index):
        return sem.at[(0,) + index], sem.at[(1,) + index]

    barrier = pltpu.get_barrier_semaphore()
    for step in range(lines):
        for core in range(2):
            if step == 0 and core == 0:
                continue
            other = base + 2 * yx + lax.rem(c + core, 2)
            pl.semaphore_signal(
                barrier,
                1,
                device_id=at(other, lax.rem(t + step, lines)),
                device_id_type=pl.DeviceIdType.MESH,
            )
    for dev in (dev_first, dev_second):
        pl.semaphore_signal(barrier, 1, device_id=dev, device_id_type=pl.DeviceIdType.MESH)
    pl.semaphore_wait(barrier, 2 * lines - 1 + 2)

    def to_owner(src, dst, sem, m, h):
        here = jnp.logical_and(t == 2 * c + m, c == t // 2)
        place = lax.rem(t, 2)
        dev = at(base + 2 * yx + t // 2, 2 * c + m)
        rows = pl.ds(128 * h, 128)
        out, into = src.at[m, rows], dst.at[place, rows]

        @pl.when(here)
        def _():
            pltpu.make_async_copy(out, into, sem.at[1, place, h]).start()

        @pl.when(jnp.logical_not(here))
        def _():
            remote(out, into, (sem.at[0, m, h], sem.at[1, place, h]), dev).start()

    def to_owner_wait(src, dst, sem):
        for k in range(2):
            for h in range(2):
                ref = dst.at[k, pl.ds(128 * h, 128)]
                pltpu.make_async_copy(ref, ref, sem.at[1, k, h]).wait()

    def to_owner_sent(src, sem):
        for m in range(2):
            here = jnp.logical_and(t == 2 * c + m, c == t // 2)

            @pl.when(jnp.logical_not(here))
            def _():
                for h in range(2):
                    ref = src.at[m, pl.ds(128 * h, 128)]
                    remote(ref, ref, (sem.at[0, m, h], sem.at[1, m, h]), dev_core).wait_send()

    def piece(i, s, place):
        return w_of[i].at[s, place, c]

    def z_right(i, src):
        slot = 2 - t // 2
        return remote(
            src, w_of[i].at[slot, yx, c], (s_zs.at[i, 0], s_zr.at[i, slot]), at(d, t + 1)
        )

    def z_left(i, src):
        return remote(src, w_of[i].at[1, yx, c], (s_zs.at[i, 1], s_zr.at[i, 1]), at(d, t - 1))

    def z_own(i):
        for copy in own[2 * i : 2 * i + 2]:
            copy.wait()
        pl.when(t < lines - 1)(lambda: z_right(i, own_piece[i]).start())
        pl.when(t > 0)(lambda: z_left(i, own_piece[i]).start())

    def z_forward(i, s):
        slot = (0, t + 1, 4 - t, 3)[s]
        line = (0, t - 1, t + 1, 3 * t - 3)[s]
        src = piece(i, s, yx)
        return remote(
            src, w_of[i].at[slot, yx, c], (s_zs.at[i, 1 + s], s_zr.at[i, slot]), at(d, line)
        )

    def z_got(i, s):
        ref = piece(i, s, yx)
        remote(ref, ref, (s_zs.at[i, 1 + s], s_zr.at[i, s]), dev_core).wait_recv()

    def z_pass(i, s):
        @pl.when(inner)
        def _():
            z_got(i, s)
            z_forward(i, s).start()

    def z_sent(i, s):
        if s == 0:
            pl.when(t < lines - 1)(lambda: z_right(i, own_piece[i]).wait_send())
            pl.when(t > 0)(lambda: z_left(i, own_piece[i]).wait_send())
        else:
            pl.when(inner)(lambda: z_forward(i, s).wait_send())

    def gather_1(i, s):
        ref = piece(i, s, yx)
        return remote(ref, ref, pair(s_1, i, s - 1), dev_first)

    def gather_2(i, s, k):
        ref = piece(i, s, yx if k == 0 else yx_first)
        return remote(ref, ref, pair(s_2, i, s - 1, k), dev_second)

    def gather_3(i, s):
        ref = w_of[i].at[s, :, c]
        return remote(ref, ref, pair(s_3, i, s - 1), dev_core)

    def step_1(i, s):
        pl.when(outer)(lambda: z_got(i, s))
        gather_1(i, s).start()

    def step_2(i, s):
        gather_1(i, s).wait_recv()
        gather_2(i, s, 0).start()
        gather_2(i, s, 1).start()

    def step_3(i, s):
        gather_2(i, s, 0).wait_recv()
        gather_2(i, s, 1).wait_recv()
        gather_3(i, s).start()

    def step_4(i, s):
        gather_3(i, s).wait()
        gather_1(i, s).wait_send()
        gather_2(i, s, 0).wait_send()
        gather_2(i, s, 1).wait_send()

    def add_into(dst, src):
        dst[...] = (dst[...].astype(F32) + src[...].astype(F32)).astype(BF)

    send_k = [(1 - c) * (2 * k + 1 - x_bit) + c * (2 * (1 - y_bit) + k) for k in range(2)]
    keep_k = [(1 - c) * (2 * k + x_bit) + c * (2 * y_bit + k) for k in range(2)]
    k_mine = (1 - c) * y_bit + c * x_bit

    def reduce_core(i, s):
        return remote(w_of[i].at[s, :, 1 - c], r_core[i].at[s], pair(s_c, i, s), dev_core)

    def reduce_a(i, s, k):
        return remote(piece(i, s, send_k[k]), r_a[i].at[s, k], pair(s_a, i, s, k), dev_first)

    def reduce_b(i, s):
        return remote(piece(i, s, yx_second), r_b[i].at[s], pair(s_b, i, s), dev_second)

    def reduce_z(i, s):
        line = (0, by_line(1, 2, 3, 2), by_line(1, 0, 1, 2), by_line(1, 2, 1, 2))[s]
        place = (0, by_line(3, 3, 3, 4), by_line(0, 4, 4, 1), by_line(2, 0, 1, 2))[s]
        return remote(
            piece(i, s, yx), r_z[i].at[place], (s_zgs.at[i, s], s_zgr.at[i, place]), at(d, line)
        )

    def reduce_z_got(i, place):
        ref = r_z[i].at[place]
        remote(ref, ref, (s_zgs.at[i, 1], s_zgr.at[i, place]), dev_core).wait_recv()

    def fold_1(i, s):
        reduce_core(i, s).start()

    def fold_2(i, s):
        reduce_core(i, s).wait_recv()
        for k in range(2):
            add_into(piece(i, s, send_k[k]), r_core[i].at[s, send_k[k]])
            reduce_a(i, s, k).start()
        for k in range(2):
            add_into(piece(i, s, keep_k[k]), r_core[i].at[s, keep_k[k]])

    def fold_3(i, s):
        reduce_a(i, s, 0).wait_recv()
        reduce_a(i, s, 1).wait_recv()
        add_into(piece(i, s, yx_second), r_a[i].at[s, 1 - k_mine])
        reduce_b(i, s).start()
        add_into(piece(i, s, yx), r_a[i].at[s, k_mine])

    def fold_4(i, s):
        reduce_b(i, s).wait_recv()
        add_into(piece(i, s, yx), r_b[i].at[s])
        if s > 0:
            pl.when(outer)(lambda: reduce_z(i, s).start())

    def fold_5(i, s):
        @pl.when(inner)
        def _():
            reduce_z_got(i, s - 1)
            add_into(piece(i, s, yx), r_z[i].at[s - 1])
            reduce_z(i, s).start()

    def own_total(i, m):
        ref = piece(i, 0, yx)
        return ref if i == ATT else ref.at[m]

    def spread_1(i, m):
        dst = grads_out[i][m].at[yx, c]
        return remote(own_total(i, m), dst, pair(s_g1, i + m), dev_first)

    def spread_2(i, m, k):
        if k == 0:
            dst = grads_out[i][m].at[yx, c]
            return remote(own_total(i, m), dst, pair(s_g2, i + m, 0), dev_second)
        ref = grads_out[i][m].at[yx_first, c]
        return remote(ref, ref, pair(s_g2, i + m, 1), dev_second)

    def spread_3(i, m):
        ref = grads_out[i][m].at[:, c]
        return remote(ref, ref, pair(s_g3, i + m), dev_core)

    def keep_total(i, m):
        dst = grads_out[i][m].at[yx, c] if whole_plane else grads_out[i][m]
        return pltpu.make_async_copy(own_total(i, m), dst, s_loc.at[4 + i + m])

    def total(i):
        for side, there in ((3, t > 0), (4, t < lines - 1)):

            @pl.when(there)
            def _():
                reduce_z_got(i, side)
                add_into(piece(i, 0, yx), r_z[i].at[side])

        for m in range(1 + i):
            keep_total(i, m).start()
            if whole_plane:
                spread_1(i, m).start()

    def spread_step_2(i):
        if whole_plane:
            for m in range(1 + i):
                spread_2(i, m, 0).start()
            for m in range(1 + i):
                spread_1(i, m).wait_recv()
                spread_2(i, m, 1).start()

    def spread_step_3(i):
        for m in range(1 + i):
            keep_total(i, m).wait()
            if whole_plane:
                spread_2(i, m, 0).wait_recv()
                spread_2(i, m, 1).wait_recv()
                spread_3(i, m).start()

    ids_copy = remote(ids_in, ids.at[c], pair(s_ids), dev_core)
    ids_copy.start()
    own = [
        pltpu.make_async_copy(shard_qkv, w_att.at[0, pl.ds(0, 3)], s_loc.at[0]),
        pltpu.make_async_copy(shard_out, w_att.at[0, 3], s_loc.at[3]),
        pltpu.make_async_copy(shard_up, w_ffn.at[0, :, :, 0], s_loc.at[1]),
        pltpu.make_async_copy(shard_down, w_ffn.at[0, :, :, 1], s_loc.at[2]),
    ]
    for copy in own:
        copy.start()
    own_piece = (w_att.at[0, yx, c], w_ffn.at[0, yx, c])
    bias[0, 0:1, :] = bias_up[...][None]
    bias[0, 1:2, :part] = bias_qv[0:1]
    bias[0, 1:2, part : 2 * part] = bias_qv[1:2]
    bias[0, 1:2, 2 * part :] = jnp.zeros((1, width - 2 * part), F32)

    def bias_copy(s):
        line = source[s]
        slot = (0, by_line(2, 2, 1, 1), by_line(3, 1, 1, 3), by_line(3, 2, 2, 3))[s]
        return remote(bias.at[0], bias.at[slot], (s_bias.at[0, s], s_bias.at[1, slot]), at(d, line))

    def bias_got(s):
        remote(bias.at[s], bias.at[s], (s_bias.at[0, s], s_bias.at[1, s]), dev_core).wait_recv()

    for s in range(1, lines):
        bias_copy(s).start()
    ids[pl.ds(c, 1)] = ids_in[...][None]

    def see():
        remote(ids_in, ids.at[1 - c], pair(s_ids), dev_core).wait_recv()
        row = ids[t // 2, pl.ds(lax.rem(t, 2), 1), :].astype(F32)
        low, high = row[:, :half], row[:, half:]
        first_core = c == 0
        ids_own = jnp.where(first_core, low, high)
        ids_other = jnp.where(first_core, high, low)
        for place, ids_k in enumerate((ids_own, ids_other)):
            columns = jnp.broadcast_to(ids_k, (128, half)).T
            for j in range(0, half, 128):
                mask[place, :, j : j + 128] = jnp.where(columns == ids_own[:, j : j + 128], 0.0, -1e30)

    def att_weights(s):
        return w_att[s].reshape(width, width)

    def up_weights(s):
        return w_ffn[s, :, :, 0].reshape(width, width)

    def down_weights(s):
        return w_ffn[s, :, :, 1].reshape(width, width)

    def kv_copy(s):
        return remote(kv.at[s], kvs.at[s], pair(s_kv, s), dev_core)

    def project(s):
        qkv = dot(att_weights(s)[: 3 * part], n1[...], NT)
        bias_row = bias[s, 1:2, : 2 * part]
        bias_col = jnp.broadcast_to(bias_row, (128, 2 * part)).T[:, :1]
        qt[s] = (qkv[:part] + bias_col[:part]).astype(BF)
        kv[s, 0] = qkv[part : 2 * part].astype(BF)
        kv[s, 1] = (qkv[2 * part :] + bias_col[part:]).astype(BF)
        kv_copy(s).start()

    def kvg_copy(s):
        return remote(kvs.at[s], kvg.at[s], pair(s_kvg, s), dev_core)

    def finish(s):
        kvg_copy(s).wait_recv()
        dq = qt[s]
        dkv = (kv[s].astype(F32) + kvg[s].astype(F32)).astype(BF).reshape(2 * part, half)
        ones = jnp.ones((8, half), BF)
        sums[s, 1:2, :part] = dot(ones, dq, NT)[:1]
        sums[s, 1:2, part : 2 * part] = dot(ones, dkv[part:], NT)[:1]
        sums[s, 1:2, 2 * part :] = jnp.zeros((1, width - 2 * part), F32)
        stacked = jnp.concatenate([dq, dkv], axis=0)
        acc[...] += dot(stacked, att_weights(s)[: 3 * part], TN)
        w_att[s, 0:3] = dot(stacked, n1[...], NN).astype(BF).reshape(3, 2, 96, width)
        fold_1(ATT, s)

    def sums_copy(s):
        return remote(
            sums.at[s],
            sums_z.at[t],
            (s_sz.at[0, s], s_sz.at[1, t]),
            at(d, source[s]),
        )

    def sums_got(s):
        ref = sums_z.at[source[s]]
        remote(ref, ref, (s_sz.at[0, s], s_sz.at[1, source[s]]), dev_core).wait_recv()

    dev_x = at(base + 2 * yx_x + c, t)
    dev_y = at(base + 2 * yx_y + c, t)

    def flip(k):
        return remote(
            sums_p.at[2 * k], sums_p.at[2 * k + 1], pair(s_sp, k), (dev_core, dev_x, dev_y)[k]
        )

    def sums_start():
        for s in range(1, lines):
            sums_copy(s).start()
        sums_z[pl.ds(t, 1)] = sums[0:1]

    def sums_line():
        for s in range(1, lines):
            sums_got(s)
        sums_p[0] = (sums_z[0] + sums_z[1]) + (sums_z[2] + sums_z[3])
        flip(0).start()

    def sums_plane(k):
        flip(k - 1).wait()
        sums_p[2 * k] = sums_p[2 * k - 2] + sums_p[2 * k - 1]
        flip(k).start()

    def sums_end():
        flip(2).wait()
        small_out[...] = sums_p[4] + sums_p[5]

    steps = {
        Z_OWN: z_own,
        Z_PASS: z_pass,
        STEP_1: step_1,
        STEP_2: step_2,
        STEP_3: step_3,
        FOLD_2: fold_2,
        FOLD_3: fold_3,
        FOLD_4: fold_4,
        FOLD_5: fold_5,
        TOTAL: total,
        SPREAD_2: spread_step_2,
        SPREAD_3: spread_step_3,
        FINISH: finish,
        SEE: see,
        SUMS: sums_start,
        SUMS_Z: sums_line,
        SUMS_P: sums_plane,
        SUMS_END: sums_end,
        MOVE: lambda name, *which: to_owner(*rows[name], *which),
    }
    rows = {
        X: (tokens, xb, s_x),
        G: (cotangent, gb, s_g),
        BO: (bo, block_home, s_bo),
        IG: (ig, input_home, s_ig),
    }

    def run(*where):
        for name, *which in PLAN.get(where, ()):
            steps[name](*which)

    def point(loop, j, where):
        for k in range(lines):
            if (loop, k, where) in PLAN:
                pl.when(j == k)(functools.partial(run, loop, k, where))

    run(START)
    to_owner_wait(tokens, xb, s_x)
    run(X_HERE)
    normed, _ = norm_parts(xb[...].reshape(half, width).astype(F32))
    n1[...] = (normed * gain_first + shift_first).astype(BF)
    for s in range(1, lines):
        bias_got(s)
    project(0)
    run(FIRST)

    def attend(s, carry):
        @pl.when(s < lines - 1)
        def _():
            step_4(ATT, s + 1)
            project(s + 1)

        kv_copy(s).wait_recv()
        for h in range(part // HEAD):
            rows = slice(h * HEAD, (h + 1) * HEAD)
            q = qt[s, rows, :]
            s0 = dot(kv[s, 0, rows, :].T, q, NN) * FACTOR + mask[0]
            s1 = dot(kvs[s, 0, rows, :].T, q, NN) * FACTOR + mask[1]
            top = jnp.maximum(
                jnp.max(s0, axis=0, keepdims=True), jnp.max(s1, axis=0, keepdims=True)
            )
            p0 = jnp.exp2(s0 - top)
            p1 = jnp.exp2(s1 - top)
            weight = column_sum(p0) + column_sum(p1)
            out = dot(kv[s, 1, rows, :], p0.astype(BF), NN)
            out = out + dot(kvs[s, 1, rows, :], p1.astype(BF), NN)
            ct[s, rows, :] = (out / weight).astype(BF)
            lse[s, h : h + 1, :] = top + jnp.log2(weight)
            point(ATTEND, s, h)
        return carry

    lax.fori_loop(0, lines, attend, 0)

    mid = xb[...].reshape(half, width).astype(F32) + bias_out
    for s in range(lines):
        mid = mid + dot(ct[s], att_weights(s)[3 * part :], TN)
    middle[...] = mid
    normed, _ = norm_parts(mid)
    low_normed = (normed * gain_second + shift_second).astype(BF)
    n2[...] = low_normed
    n2t[...] = low_normed.T
    acc[...] = jnp.zeros_like(acc)
    acc2[...] = jnp.zeros_like(acc2)
    run(OUT)
    to_owner_wait(cotangent, gb, s_g)

    def feed(s, carry):
        @pl.when(s > 0)
        def _():
            step_4(FFN, s)

        for k in range(lines):
            pl.when(s == k)(functools.partial(z_sent, FFN, k))
        point(FEED, s, 0)
        grad = gb[...].reshape(half, width)
        pre = dot(n2[...], up_weights(s), NN) + bias[s, 0:1, :]
        phi = 0.5 * (1.0 + lax.erf(pre * 0.7071067811865476))
        active = (pre * phi).astype(BF)
        slope = phi + pre * jnp.exp(-0.5 * pre * pre) * 0.3989422804014327
        acc[...] += dot(active, down_weights(s), NN)
        point(FEED, s, 1)
        pre_grad = (dot(grad, down_weights(s), NT) * slope).astype(BF)
        sums[s, 0:1, :] = column_sum(pre_grad.astype(F32))
        point(FEED, s, 2)
        acc2[...] += dot(pre_grad, up_weights(s), NT)
        point(FEED, s, 3)
        w_ffn[s, :, :, 1] = dot(active, grad, TN).astype(BF).reshape(4, 2, 96, width)
        point(FEED, s, 4)
        w_ffn[s, :, :, 0] = dot(n2t[...], pre_grad, NN).astype(BF).reshape(4, 2, 96, width)
        fold_1(FFN, s)
        point(FEED, s, 5)
        return carry

    lax.fori_loop(0, lines, feed, 0)

    mid = middle[...]
    bo[...] = (mid + acc[...] + bias_down).astype(BF).reshape(2, 256, width)
    run(BLOCK)
    normed, rate = norm_parts(mid)
    grad = gb[...].reshape(half, width).astype(F32)
    back = acc2[...]
    middle_grad = grad + norm_back(normed, rate, back, gain_second)
    vec_out = column_sum(middle_grad)
    vec_gain = column_sum(back * normed)
    vec_shift = column_sum(back)
    vec_down = column_sum(grad)
    for s in range(lines):
        sums[s, 4:5, :] = vec_out
        sums[s, 5:6, :] = vec_gain
        sums[s, 6:7, :] = vec_shift
        sums[s, 7:8, :] = vec_down
    acc2[...] = middle_grad
    dmr[...] = middle_grad.astype(BF)
    acc[...] = jnp.zeros_like(acc)
    for s in range(lines):
        z_sent(ATT, s)
    run(NORM)

    def attend_back(j, carry):
        s = by_line_of(j, *ORDER)
        dct = dot(w_att[s, 3].reshape(part, width), dmr[...], NT).astype(BF)
        w_att[s, 3] = dot(ct[s], dmr[...], NN).astype(BF).reshape(2, 96, width)
        kv_copy(s).wait_send()
        point(BACK, j, 0)
        for h in range(part // HEAD):
            rows = slice(h * HEAD, (h + 1) * HEAD)
            g = dct[rows]
            q = qt[s, rows, :]
            along = column_sum(g.astype(F32) * ct[s, rows, :].astype(F32))
            total_log = lse[s, h : h + 1, :]
            dq = jnp.zeros((HEAD, half), F32)
            for place, ref in enumerate((kv, kvs)):
                k = ref[s, 0, rows, :]
                v = ref[s, 1, rows, :]
                p = jnp.exp2(dot(k.T, q, NN) * FACTOR + mask[place] - total_log)
                ds = (p * (dot(v.T, g, NN) - along)).astype(BF)
                ref[s, 0, rows, :] = (dot(q, ds, NT) * HEAD**-0.5).astype(BF)
                ref[s, 1, rows, :] = dot(g, p.astype(BF), NT).astype(BF)
                dq = dq + dot(k, ds, NN)
            qt[s, rows, :] = (dq * HEAD**-0.5).astype(BF)
            if h == part // HEAD - 1:
                kvg_copy(s).start()
            point(BACK, j, h + 1)
        return carry

    lax.fori_loop(0, lines, attend_back, 0)
    run(TAIL_0)

    normed, rate = norm_parts(xb[...].reshape(half, width).astype(F32))
    back = acc[...]
    vec_gain = column_sum(back * normed)
    vec_shift = column_sum(back)
    for s in range(lines):
        sums[s, 2:3, :] = vec_gain
        sums[s, 3:4, :] = vec_shift

    run(TAIL_1)
    ig[...] = (
        (acc2[...] + norm_back(normed, rate, back, gain_first))
        .astype(BF)
        .reshape(2, 256, width)
    )
    run(TAIL_2)
    run(TAIL_3)

    ids_copy.wait_send()
    for s in range(1, lines):
        bias_copy(s).wait_send()
        sums_copy(s).wait_send()
    to_owner_sent(tokens, s_x)
    to_owner_sent(cotangent, s_g)
    to_owner_wait(bo, block_home, s_bo)
    to_owner_sent(bo, s_bo)
    for s in range(lines):
        kvg_copy(s).wait_send()
    for i in (ATT, FFN):
        for s in range(lines):
            reduce_core(i, s).wait_send()
            reduce_a(i, s, 0).wait_send()
            reduce_a(i, s, 1).wait_send()
            reduce_b(i, s).wait_send()
            if s > 0:
                reduce_z(i, s).wait_send()
        for m in range(1 + i if whole_plane else 0):
            spread_1(i, m).wait_send()
            spread_2(i, m, 0).wait_send()
            spread_2(i, m, 1).wait_send()
            spread_3(i, m).wait()
    to_owner_wait(ig, input_home, s_ig)
    to_owner_sent(ig, s_ig)


def layer(lines, whole_plane, operands):
    def dma(*shape):
        return pltpu.SemaphoreType.DMA((2,) + shape)

    def vmem(*shape, dtype=BF):
        return pltpu.VMEM(shape, dtype)

    n = lines
    anywhere = pl.BlockSpec(memory_space=pl.ANY)
    inside = pl.BlockSpec(memory_space=pltpu.VMEM)
    att = (96, 768)
    ffn = (2, 96, 768)
    plane = (4, 2) if whole_plane else ()
    blocks = jax.ShapeDtypeStruct((2, 256, 768), BF)
    return pl.pallas_call(
        functools.partial(layer_kernel, lines, whole_plane),
        in_specs=[anywhere, anywhere, inside] + [anywhere] * 4 + [inside] * 8,
        out_specs=[anywhere] * 5 + [inside],
        out_shape=[
            blocks,
            blocks,
            jax.ShapeDtypeStruct(plane + att, BF),
            jax.ShapeDtypeStruct(plane + att, BF),
            jax.ShapeDtypeStruct(plane + att, BF),
            jax.ShapeDtypeStruct((8, 768), F32),
        ],
        scratch_shapes=[
            vmem(n, 4, 2, *att),
            vmem(n, 4, 2, *ffn),
            vmem(n, 4, *att),
            vmem(n, 4, *ffn),
            vmem(n, 2, *att),
            vmem(n, 2, *ffn),
            vmem(n, *att),
            vmem(n, *ffn),
            vmem(5, *att),
            vmem(5, *ffn),
            vmem(2, 256, 768),
            vmem(2, 256, 768),
            vmem(2, 2, 1024, dtype=jnp.int32),
            vmem(n, 8, 768, dtype=F32),
            vmem(2, 512, 512, dtype=F32),
            vmem(512, 768),
            vmem(512, 768),
            vmem(768, 512),
            vmem(512, 768, dtype=F32),
            vmem(512, 768, dtype=F32),
            vmem(512, 768, dtype=F32),
            vmem(512, 768),
            vmem(n, 192, 512),
            vmem(n, 2, 192, 512),
            vmem(n, 2, 192, 512),
            vmem(n, 2, 192, 512),
            vmem(n, 192, 512),
            vmem(n, 8, 512, dtype=F32),
            vmem(2, 256, 768),
            vmem(2, 256, 768),
            vmem(n, 8, 768, dtype=F32),
            vmem(n, 8, 768, dtype=F32),
            vmem(6, 8, 768, dtype=F32),
            pltpu.SemaphoreType.DMA((7,)),
            dma(),
            dma(n),
            dma(2, 2),
            dma(2, 2),
            dma(2, 2),
            dma(2, 2),
            dma(n),
            dma(n),
            pltpu.SemaphoreType.DMA((2, 5)),
            pltpu.SemaphoreType.DMA((2, n)),
            dma(2, n - 1),
            dma(2, n - 1, 2),
            dma(2, n - 1),
            dma(2, n),
            dma(2, n, 2),
            dma(2, n),
            pltpu.SemaphoreType.DMA((2, n)),
            pltpu.SemaphoreType.DMA((2, 5)),
            dma(3),
            dma(3, 2),
            dma(3),
            dma(n),
            dma(3),
        ],
        compiler_params=pltpu.CompilerParams(
            collective_id=0, has_side_effects=True, vmem_limit_bytes=62 * 2**20
        ),
        name="layer",
    )(*operands)


def results_kernel(
    block_in, input_in, att_in, up_in, down_in, small_in,
    block_out, input_out, qkv_out, out_out, up_out, down_out, bias_out, *rest
):
    sums_out, (low_in, low_att, low_up, low_down) = rest[:7], rest[7:11]
    wide_in, wide_att, wide_up, wide_down, low_block, s_in, s_out, s_block = rest[11:]
    part = bias_out.shape[1]
    third = 3 * part
    block = pltpu.make_async_copy(block_in, low_block, s_block)
    jobs = [(up_in, low_up, wide_up, up_out, 0, 0, 2 * part)]
    jobs += [(up_in, low_up, wide_up, up_out, 2 * part, 2 * part, 2 * part)]
    jobs += [(down_in, low_down, wide_down, down_out, k, k, 2 * part) for k in (0, 2 * part)]
    jobs += [(att_in, low_att, wide_att, qkv_out, 0, 0, third)]
    jobs += [(att_in, low_att, wide_att, out_out, third, 0, part)]
    jobs += [(input_in, low_in, wide_in, input_out, k, k, 256) for k in (0, 256)]

    def fetch(k):
        source, low, _, _, at, _, size = jobs[k]
        rows = pl.ds(at, size)
        return pltpu.make_async_copy(source.at[rows], low.at[rows], s_in.at[k])

    def store(k):
        _, _, wide, result, at, to, size = jobs[k]
        return pltpu.make_async_copy(wide.at[pl.ds(at, size)], result.at[pl.ds(to, size)], s_out.at[k])

    for k in range(len(jobs)):
        fetch(k).start()
    block.start()
    bias_out[0:1] = small_in[1:2, :part]
    bias_out[1:2] = small_in[1:2, part : 2 * part]
    for ref, row in zip(sums_out, (0, 2, 3, 4, 5, 6, 7)):
        ref[...] = small_in[row]
    for k, (_, low, wide, _, at, _, size) in enumerate(jobs):
        fetch(k).wait()
        wide[pl.ds(at, size)] = low[pl.ds(at, size)].astype(F32)
        store(k).start()
    block.wait()
    block = pltpu.make_async_copy(low_block, block_out, s_block)
    block.start()
    for k in range(len(jobs)):
        store(k).wait()
    block.wait()


def results(block, inputs, att, up, down, small):
    width = att.shape[0]
    part = width // 4
    tokens = inputs.shape[0] * inputs.shape[1]
    anywhere = pl.BlockSpec(memory_space=pl.ANY)
    inside = pl.BlockSpec(memory_space=pltpu.VMEM)
    shapes = ((tokens, width), (width, width), (width, width), (width, width))
    block, inputs, *results = pl.pallas_call(
        results_kernel,
        in_specs=[anywhere] * 5 + [inside],
        out_specs=[anywhere] * 6 + [inside] * 8,
        out_shape=[
            jax.ShapeDtypeStruct(block.shape, BF),
            jax.ShapeDtypeStruct((tokens, width), F32),
            jax.ShapeDtypeStruct((3 * part, width), F32),
            jax.ShapeDtypeStruct((part, width), F32),
            jax.ShapeDtypeStruct((width, width), F32),
            jax.ShapeDtypeStruct((width, width), F32),
            jax.ShapeDtypeStruct((2, part), F32),
        ]
        + [jax.ShapeDtypeStruct((width,), F32)] * 7,
        scratch_shapes=[pltpu.VMEM(shape, BF) for shape in shapes]
        + [pltpu.VMEM(shape, F32) for shape in shapes]
        + [pltpu.VMEM(block.shape, BF)]
        + [pltpu.SemaphoreType.DMA((8,)), pltpu.SemaphoreType.DMA((8,)), pltpu.SemaphoreType.DMA],
        compiler_params=pltpu.CompilerParams(vmem_limit_bytes=62 * 2**20),
        name="results",
    )(block, inputs.reshape(tokens, width), att, up, down, small)
    return (block, inputs.reshape(block.shape), *results)


def body(
    dp,
    lines,
    tokens,
    segment_ids,
    gain_first,
    shift_first,
    weight_qkv,
    bias_qv,
    weight_out,
    bias_out,
    gain_second,
    shift_second,
    weight_up,
    bias_up,
    weight_down,
    bias_down,
    cotangent,
):
    width = tokens.shape[2]
    part = weight_qkv.shape[2]
    shard = (4, 2, width // PLANE, width)
    whole_plane = dp == PLANE
    block_out, input_grad, *grads, small = layer(
        lines,
        whole_plane,
        (
            tokens,
            cotangent,
            segment_ids,
            weight_qkv.reshape(width, 3 * part).T.reshape(3, 2, width // PLANE, width),
            weight_out.reshape(2, width // PLANE, width),
            weight_up.reshape(shard),
            weight_down.reshape(shard),
            bias_up,
            bias_qv,
            gain_first,
            shift_first,
            bias_out,
            gain_second,
            shift_second,
            bias_down,
        ),
    )
    if not whole_plane:
        apart = [[i + PLANE * g for g in range(dp // PLANE)] for i in range(PLANE)]
        planes = [[i + PLANE * g for i in range(PLANE)] for g in range(dp // PLANE)]
        sums = tuple(grad.astype(F32) for grad in grads)
        *grads, small = lax.psum(sums + (small,), "dp", axis_index_groups=apart)
        grads = [lax.all_gather(g.astype(BF), "dp", axis_index_groups=planes) for g in grads]
    att_grad, up_grad, down_grad = [grad.reshape(width, width) for grad in grads]
    block_out, input_grad, qkv_grad, out_grad, up_grad, down_grad, bias_grad, *sums = results(
        block_out, input_grad, att_grad, up_grad, down_grad, small
    )
    up_bias, gain_one, shift_one, out_bias, gain_two, shift_two, down_bias = sums
    return (
        block_out,
        input_grad,
        gain_one,
        shift_one,
        qkv_grad.T.reshape(width, 3, part),
        bias_grad,
        out_grad,
        out_bias,
        gain_two,
        shift_two,
        up_grad,
        up_bias,
        down_grad,
        down_bias,
    )


def solution(mesh):
    in_specs = (
        P("dp", "tensor", None),
        P("dp", None),
        P(),
        P(),
        P(None, None, "tensor"),
        P(None, "tensor"),
        P("tensor", None),
        P(),
        P(),
        P(),
        P(None, "tensor"),
        P("tensor"),
        P("tensor", None),
        P(),
        P("dp", "tensor", None),
    )
    out_specs = (
        P("dp", "tensor", None),
        P("dp", "tensor", None),
        P(),
        P(),
        P(None, None, "tensor"),
        P(None, "tensor"),
        P("tensor", None),
        P(),
        P(),
        P(),
        P(None, "tensor"),
        P("tensor"),
        P("tensor", None),
        P(),
    )
    whole = functools.partial(body, mesh.shape["dp"], mesh.shape["tensor"])
    return jax.shard_map(whole, mesh=mesh, in_specs=in_specs, out_specs=out_specs, check_vma=False)
```

```python
import functools

import jax
import jax.numpy as jnp
from jax import lax
from jax.experimental import pallas as pl
from jax.experimental.pallas import tpu as pltpu
from jax.sharding import PartitionSpec as P

HEAD = 64
PLANE = 8
FACTOR = HEAD**-0.5 * 1.4426950408889634
BF = jnp.bfloat16
F32 = jnp.float32
NN = ((1,), (0,))
NT = ((1,), (1,))
TN = ((0,), (0,))
ATT, FFN = 0, 1

Z_OWN, Z_PASS, STEP_1, STEP_2, STEP_3, FOLD_2, FOLD_3, FOLD_4, FOLD_5, TOTAL = range(10)
SPREAD_2, SPREAD_3, FINISH, SEE, SUMS, SUMS_Z, SUMS_P, SUMS_END, MOVE = range(10, 19)
X, G, BO, IG = range(4)
START, X_HERE, FIRST, ATTEND, OUT, FEED, BLOCK, NORM, BACK, TAIL_0, TAIL_1, TAIL_2, TAIL_3 = range(13)

ORDER = (3, 2, 1, 0)

PLAN = {
    (START,): (
        (Z_OWN, ATT),
        (MOVE, X, 0, 0),
        (MOVE, X, 1, 1),
        (Z_PASS, ATT, 1),
        (Z_PASS, ATT, 2),
        (STEP_1, ATT, 1),
        (Z_OWN, FFN),
        (STEP_1, ATT, 2),
        (STEP_2, ATT, 1),
        (Z_PASS, ATT, 3),
        (MOVE, X, 0, 1),
        (MOVE, X, 1, 0),
        (STEP_1, ATT, 3),
        (SEE,),
        (Z_PASS, FFN, 1),
        (STEP_1, FFN, 1),
        (STEP_2, ATT, 2),
    ),
    (X_HERE,): (
        (MOVE, G, 0, 0),
        (Z_PASS, FFN, 2),
        (STEP_3, ATT, 1),
        (STEP_2, ATT, 3),
    ),
    (FIRST,): (
        (STEP_3, ATT, 2),
        (STEP_1, FFN, 2),
    ),
    (ATTEND, 0, 0): (
        (STEP_2, FFN, 1),
        (MOVE, G, 1, 0),
    ),
    (ATTEND, 1, 0): (
        (Z_PASS, FFN, 3),
        (MOVE, G, 1, 1),
    ),
    (ATTEND, 1, 2): (
        (STEP_3, ATT, 3),
        (STEP_2, FFN, 2),
        (MOVE, G, 0, 1),
    ),
    (ATTEND, 2, 2): (
        (STEP_3, FFN, 1),
    ),
    (ATTEND, 3, 2): (
        (STEP_1, FFN, 3),
    ),
    (FEED, 0, 3): (
        (STEP_3, FFN, 2),
        (STEP_2, FFN, 3),
    ),
    (FEED, 2, 1): (
        (FOLD_2, FFN, 0),
        (STEP_3, FFN, 3),
    ),
    (FEED, 2, 3): (
        (FOLD_2, FFN, 1),
    ),
    (BLOCK,): (
        (MOVE, BO, 1, 1),
    ),
    (BACK, 0, 1): (
        (FOLD_2, FFN, 3),
    ),
    (BACK, 0, 3): (
        (MOVE, BO, 1, 0),
    ),
    (BACK, 1, 0): (
        (MOVE, BO, 0, 0),
        (FOLD_2, FFN, 2),
    ),
    (BACK, 1, 1): (
        (FINISH, 3),
        (FOLD_3, FFN, 3),
    ),
    (BACK, 1, 2): (
        (FOLD_2, ATT, 3),
    ),
    (BACK, 1, 3): (
        (MOVE, BO, 0, 1),
        (FINISH, 2),
    ),
    (BACK, 2, 0): (
        (FOLD_4, FFN, 3),
    ),
    (BACK, 2, 1): (
        (FOLD_3, FFN, 2),
    ),
    (BACK, 3, 0): (
        (FOLD_3, ATT, 3),
        (FOLD_3, FFN, 1),
    ),
    (BACK, 3, 1): (
        (FOLD_4, FFN, 2),
        (FOLD_5, FFN, 3),
        (FOLD_2, ATT, 2),
    ),
    (BACK, 3, 2): (
        (FINISH, 1),
        (FOLD_3, FFN, 0),
    ),
    (BACK, 3, 3): (
        (FOLD_4, ATT, 3),
        (FOLD_4, FFN, 1),
        (FOLD_2, ATT, 1),
        (FOLD_5, FFN, 2),
        (FOLD_5, FFN, 1),
    ),
    (TAIL_0,): (
        (FINISH, 0),
        (FOLD_3, ATT, 2),
    ),
    (TAIL_1,): (
        (FOLD_2, ATT, 0),
        (FOLD_5, ATT, 3),
        (FOLD_3, ATT, 1),
    ),
    (TAIL_2,): (
        (FOLD_4, FFN, 0),
        (FOLD_4, ATT, 2),
        (SUMS,),
        (MOVE, IG, 1, 0),
        (TOTAL, FFN),
        (FOLD_3, ATT, 0),
        (FOLD_4, ATT, 1),
        (FOLD_5, ATT, 2),
        (SUMS_Z,),
        (MOVE, IG, 0, 1),
    ),
    (TAIL_3,): (
        (FOLD_4, ATT, 0),
        (FOLD_5, ATT, 1),
        (SUMS_P, 1),
        (SPREAD_2, FFN),
        (MOVE, IG, 1, 1),
        (TOTAL, ATT),
        (MOVE, IG, 0, 0),
        (SPREAD_2, ATT),
        (SUMS_P, 2),
        (SPREAD_3, FFN),
        (SPREAD_3, ATT),
        (SUMS_END,),
    ),
}


def dot(left, right, dims):
    return lax.dot_general(left, right, (dims, ((), ())), preferred_element_type=F32)


def norm_parts(values):
    center = values - jnp.mean(values, axis=-1, keepdims=True)
    rate = lax.rsqrt(jnp.mean(center * center, axis=-1, keepdims=True) + 1e-5)
    return center * rate, rate


def norm_back(normed, rate, grad, gain):
    scaled = grad * gain
    mean = jnp.mean(scaled, axis=-1, keepdims=True)
    along = jnp.mean(scaled * normed, axis=-1, keepdims=True)
    return rate * (scaled - mean - normed * along)


def column_sum(values):
    return jnp.sum(values, axis=0, keepdims=True)


def layer_kernel(
    lines,
    whole_plane,
    tokens,
    cotangent,
    ids_in,
    shard_qkv,
    shard_out,
    shard_up,
    shard_down,
    bias_up,
    bias_qv,
    gain_first,
    shift_first,
    bias_out,
    gain_second,
    shift_second,
    bias_down,
    block_home,
    input_home,
    grads_att,
    grads_up,
    grads_down,
    small_out,
    w_att,
    w_ffn,
    r_core_att,
    r_core_ffn,
    r_a_att,
    r_a_ffn,
    r_b_att,
    r_b_ffn,
    r_z_att,
    r_z_ffn,
    xb,
    gb,
    ids,
    bias,
    mask,
    n1,
    n2,
    n2t,
    middle,
    acc,
    acc2,
    dmr,
    qt,
    kv,
    kvs,
    kvg,
    ct,
    lse,
    bo,
    ig,
    sums,
    sums_z,
    sums_p,
    s_loc,
    s_ids,
    s_bias,
    s_x,
    s_g,
    s_bo,
    s_ig,
    s_kv,
    s_kvg,
    s_zs,
    s_zr,
    s_1,
    s_2,
    s_3,
    s_c,
    s_a,
    s_b,
    s_zgs,
    s_zgr,
    s_g1,
    s_g2,
    s_g3,
    s_sz,
    s_sp,
):
    t = lax.axis_index("tensor")
    d = lax.axis_index("dp")
    e = lax.rem(d, PLANE)
    base = d - e
    c = lax.rem(e, 2)
    yx = e // 2
    x_bit = lax.rem(yx, 2)
    y_bit = yx // 2
    half = 512
    part = 192
    width = 768
    w_of = (w_att, w_ffn)
    r_core = (r_core_att, r_core_ffn)
    r_a = (r_a_att, r_a_ffn)
    r_b = (r_b_att, r_b_ffn)
    r_z = (r_z_att, r_z_ffn)
    grads_out = ((grads_att,), (grads_up, grads_down))
    gain_first, shift_first, bias_out = [r[...][None] for r in (gain_first, shift_first, bias_out)]
    gain_second, shift_second = gain_second[...][None], shift_second[...][None]
    bias_down = bias_down[...][None]

    yx_x = 2 * y_bit + 1 - x_bit
    yx_y = 2 * (1 - y_bit) + x_bit
    yx_first = (1 - c) * yx_x + c * yx_y
    yx_second = (1 - c) * yx_y + c * yx_x

    def at(dp_index, line):
        return {"dp": dp_index, "tensor": line}

    dev_core = at(base + 2 * yx + 1 - c, t)
    dev_first = at(base + 2 * yx_first + c, t)
    dev_second = at(base + 2 * yx_second + c, t)

    def by_line_of(place, *values):
        out = values[3]
        for k in (2, 1, 0):
            out = jnp.where(place == k, values[k], out)
        return out

    def by_line(*values):
        return by_line_of(t, *values)

    source = [t, by_line(1, 2, 3, 2), by_line(2, 0, 1, 1), by_line(3, 3, 0, 0)]
    inner = jnp.logical_and(t > 0, t < lines - 1)
    outer = jnp.logical_not(inner)

    def remote(src, dst, sems, dev):
        return pltpu.make_async_remote_copy(
            src_ref=src,
            dst_ref=dst,
            send_sem=sems[0],
            recv_sem=sems[1],
            device_id=dev,
            device_id_type=pl.DeviceIdType.MESH,
        )

    def pair(sem, *index):
        return sem.at[(0,) + index], sem.at[(1,) + index]

    barrier = pltpu.get_barrier_semaphore()
    for step in range(lines):
        for core in range(2):
            if step == 0 and core == 0:
                continue
            other = base + 2 * yx + lax.rem(c + core, 2)
            pl.semaphore_signal(
                barrier,
                1,
                device_id=at(other, lax.rem(t + step, lines)),
                device_id_type=pl.DeviceIdType.MESH,
            )
    for dev in (dev_first, dev_second):
        pl.semaphore_signal(barrier, 1, device_id=dev, device_id_type=pl.DeviceIdType.MESH)
    pl.semaphore_wait(barrier, 2 * lines - 1 + 2)

    def to_owner(src, dst, sem, m, h):
        here = jnp.logical_and(t == 2 * c + m, c == t // 2)
        place = lax.rem(t, 2)
        dev = at(base + 2 * yx + t // 2, 2 * c + m)
        rows = pl.ds(128 * h, 128)
        out, into = src.at[m, rows], dst.at[place, rows]

        @pl.when(here)
        def _():
            pltpu.make_async_copy(out, into, sem.at[1, place, h]).start()

        @pl.when(jnp.logical_not(here))
        def _():
            remote(out, into, (sem.at[0, m, h], sem.at[1, place, h]), dev).start()

    def to_owner_wait(src, dst, sem):
        for k in range(2):
            for h in range(2):
                ref = dst.at[k, pl.ds(128 * h, 128)]
                pltpu.make_async_copy(ref, ref, sem.at[1, k, h]).wait()

    def to_owner_sent(src, sem):
        for m in range(2):
            here = jnp.logical_and(t == 2 * c + m, c == t // 2)

            @pl.when(jnp.logical_not(here))
            def _():
                for h in range(2):
                    ref = src.at[m, pl.ds(128 * h, 128)]
                    remote(ref, ref, (sem.at[0, m, h], sem.at[1, m, h]), dev_core).wait_send()

    def piece(i, s, place):
        return w_of[i].at[s, place, c]

    def z_right(i, src):
        slot = 2 - t // 2
        return remote(
            src, w_of[i].at[slot, yx, c], (s_zs.at[i, 0], s_zr.at[i, slot]), at(d, t + 1)
        )

    def z_left(i, src):
        return remote(src, w_of[i].at[1, yx, c], (s_zs.at[i, 1], s_zr.at[i, 1]), at(d, t - 1))

    def z_own(i):
        for copy in own[2 * i : 2 * i + 2]:
            copy.wait()
        pl.when(t < lines - 1)(lambda: z_right(i, own_piece[i]).start())
        pl.when(t > 0)(lambda: z_left(i, own_piece[i]).start())

    def z_forward(i, s):
        slot = (0, t + 1, 4 - t, 3)[s]
        line = (0, t - 1, t + 1, 3 * t - 3)[s]
        src = piece(i, s, yx)
        return remote(
            src, w_of[i].at[slot, yx, c], (s_zs.at[i, 1 + s], s_zr.at[i, slot]), at(d, line)
        )

    def z_got(i, s):
        ref = piece(i, s, yx)
        remote(ref, ref, (s_zs.at[i, 1 + s], s_zr.at[i, s]), dev_core).wait_recv()

    def z_pass(i, s):
        @pl.when(inner)
        def _():
            z_got(i, s)
            z_forward(i, s).start()

    def z_sent(i, s):
        if s == 0:
            pl.when(t < lines - 1)(lambda: z_right(i, own_piece[i]).wait_send())
            pl.when(t > 0)(lambda: z_left(i, own_piece[i]).wait_send())
        else:
            pl.when(inner)(lambda: z_forward(i, s).wait_send())

    def gather_1(i, s):
        ref = piece(i, s, yx)
        return remote(ref, ref, pair(s_1, i, s - 1), dev_first)

    def gather_2(i, s, k):
        ref = piece(i, s, yx if k == 0 else yx_first)
        return remote(ref, ref, pair(s_2, i, s - 1, k), dev_second)

    def gather_3(i, s):
        ref = w_of[i].at[s, :, c]
        return remote(ref, ref, pair(s_3, i, s - 1), dev_core)

    def step_1(i, s):
        pl.when(outer)(lambda: z_got(i, s))
        gather_1(i, s).start()

    def step_2(i, s):
        gather_1(i, s).wait_recv()
        gather_2(i, s, 0).start()
        gather_2(i, s, 1).start()

    def step_3(i, s):
        gather_2(i, s, 0).wait_recv()
        gather_2(i, s, 1).wait_recv()
        gather_3(i, s).start()

    def step_4(i, s):
        gather_3(i, s).wait()
        gather_1(i, s).wait_send()
        gather_2(i, s, 0).wait_send()
        gather_2(i, s, 1).wait_send()

    def add_into(dst, src):
        dst[...] = dst[...] + src[...]

    send_k = [(1 - c) * (2 * k + 1 - x_bit) + c * (2 * (1 - y_bit) + k) for k in range(2)]
    keep_k = [(1 - c) * (2 * k + x_bit) + c * (2 * y_bit + k) for k in range(2)]
    k_mine = (1 - c) * y_bit + c * x_bit

    def reduce_core(i, s):
        return remote(w_of[i].at[s, :, 1 - c], r_core[i].at[s], pair(s_c, i, s), dev_core)

    def reduce_a(i, s, k):
        return remote(piece(i, s, send_k[k]), r_a[i].at[s, k], pair(s_a, i, s, k), dev_first)

    def reduce_b(i, s):
        return remote(piece(i, s, yx_second), r_b[i].at[s], pair(s_b, i, s), dev_second)

    def reduce_z(i, s):
        line = (0, by_line(1, 2, 3, 2), by_line(1, 0, 1, 2), by_line(1, 2, 1, 2))[s]
        place = (0, by_line(3, 3, 3, 4), by_line(0, 4, 4, 1), by_line(2, 0, 1, 2))[s]
        return remote(
            piece(i, s, yx), r_z[i].at[place], (s_zgs.at[i, s], s_zgr.at[i, place]), at(d, line)
        )

    def reduce_z_got(i, place):
        ref = r_z[i].at[place]
        remote(ref, ref, (s_zgs.at[i, 1], s_zgr.at[i, place]), dev_core).wait_recv()

    def fold_1(i, s):
        reduce_core(i, s).start()

    def fold_2(i, s):
        reduce_core(i, s).wait_recv()
        for k in range(2):
            add_into(piece(i, s, send_k[k]), r_core[i].at[s, send_k[k]])
            reduce_a(i, s, k).start()
        for k in range(2):
            add_into(piece(i, s, keep_k[k]), r_core[i].at[s, keep_k[k]])

    def fold_3(i, s):
        reduce_a(i, s, 0).wait_recv()
        reduce_a(i, s, 1).wait_recv()
        add_into(piece(i, s, yx_second), r_a[i].at[s, 1 - k_mine])
        reduce_b(i, s).start()
        add_into(piece(i, s, yx), r_a[i].at[s, k_mine])

    def fold_4(i, s):
        reduce_b(i, s).wait_recv()
        add_into(piece(i, s, yx), r_b[i].at[s])
        if s > 0:
            pl.when(outer)(lambda: reduce_z(i, s).start())

    def fold_5(i, s):
        @pl.when(inner)
        def _():
            reduce_z_got(i, s - 1)
            add_into(piece(i, s, yx), r_z[i].at[s - 1])
            reduce_z(i, s).start()

    def own_total(i, m):
        ref = piece(i, 0, yx)
        return ref if i == ATT else ref.at[m]

    def spread_1(i, m):
        dst = grads_out[i][m].at[yx, c]
        return remote(own_total(i, m), dst, pair(s_g1, i + m), dev_first)

    def spread_2(i, m, k):
        if k == 0:
            dst = grads_out[i][m].at[yx, c]
            return remote(own_total(i, m), dst, pair(s_g2, i + m, 0), dev_second)
        ref = grads_out[i][m].at[yx_first, c]
        return remote(ref, ref, pair(s_g2, i + m, 1), dev_second)

    def spread_3(i, m):
        ref = grads_out[i][m].at[:, c]
        return remote(ref, ref, pair(s_g3, i + m), dev_core)

    def keep_total(i, m):
        dst = grads_out[i][m].at[yx, c] if whole_plane else grads_out[i][m]
        return pltpu.make_async_copy(own_total(i, m), dst, s_loc.at[4 + i + m])

    def total(i):
        for side, there in ((3, t > 0), (4, t < lines - 1)):

            @pl.when(there)
            def _():
                reduce_z_got(i, side)
                add_into(piece(i, 0, yx), r_z[i].at[side])

        for m in range(1 + i):
            keep_total(i, m).start()
            if whole_plane:
                spread_1(i, m).start()

    def spread_step_2(i):
        if whole_plane:
            for m in range(1 + i):
                spread_2(i, m, 0).start()
            for m in range(1 + i):
                spread_1(i, m).wait_recv()
                spread_2(i, m, 1).start()

    def spread_step_3(i):
        for m in range(1 + i):
            keep_total(i, m).wait()
            if whole_plane:
                spread_2(i, m, 0).wait_recv()
                spread_2(i, m, 1).wait_recv()
                spread_3(i, m).start()

    ids_copy = remote(ids_in, ids.at[c], pair(s_ids), dev_core)
    ids_copy.start()
    own = [
        pltpu.make_async_copy(shard_qkv, w_att.at[0, pl.ds(0, 3)], s_loc.at[0]),
        pltpu.make_async_copy(shard_out, w_att.at[0, 3], s_loc.at[3]),
        pltpu.make_async_copy(shard_up, w_ffn.at[0, :, :, 0], s_loc.at[1]),
        pltpu.make_async_copy(shard_down, w_ffn.at[0, :, :, 1], s_loc.at[2]),
    ]
    for copy in own:
        copy.start()
    own_piece = (w_att.at[0, yx, c], w_ffn.at[0, yx, c])
    bias[0, 0:1, :] = bias_up[...][None]
    bias[0, 1:2, :part] = bias_qv[0:1]
    bias[0, 1:2, part : 2 * part] = bias_qv[1:2]
    bias[0, 1:2, 2 * part :] = jnp.zeros((1, width - 2 * part), F32)

    def bias_copy(s):
        line = source[s]
        slot = (0, by_line(2, 2, 1, 1), by_line(3, 1, 1, 3), by_line(3, 2, 2, 3))[s]
        return remote(bias.at[0], bias.at[slot], (s_bias.at[0, s], s_bias.at[1, slot]), at(d, line))

    def bias_got(s):
        remote(bias.at[s], bias.at[s], (s_bias.at[0, s], s_bias.at[1, s]), dev_core).wait_recv()

    for s in range(1, lines):
        bias_copy(s).start()
    ids[pl.ds(c, 1)] = ids_in[...][None]

    def see():
        remote(ids_in, ids.at[1 - c], pair(s_ids), dev_core).wait_recv()
        row = ids[t // 2, pl.ds(lax.rem(t, 2), 1), :].astype(F32)
        low, high = row[:, :half], row[:, half:]
        first_core = c == 0
        ids_own = jnp.where(first_core, low, high)
        ids_other = jnp.where(first_core, high, low)
        for place, ids_k in enumerate((ids_own, ids_other)):
            columns = jnp.broadcast_to(ids_k, (128, half)).T
            for j in range(0, half, 128):
                mask[place, :, j : j + 128] = jnp.where(columns == ids_own[:, j : j + 128], 0.0, -1e30)

    def att_weights(s):
        return w_att[s].reshape(width, width)

    def up_weights(s):
        return w_ffn[s, :, :, 0].reshape(width, width)

    def down_weights(s):
        return w_ffn[s, :, :, 1].reshape(width, width)

    def kv_copy(s):
        return remote(kv.at[s], kvs.at[s], pair(s_kv, s), dev_core)

    def project(s):
        qkv = dot(att_weights(s)[: 3 * part], n1[...], NT)
        bias_row = bias[s, 1:2, : 2 * part]
        bias_col = jnp.broadcast_to(bias_row, (128, 2 * part)).T[:, :1]
        qt[s] = (qkv[:part] + bias_col[:part]).astype(BF)
        kv[s, 0] = qkv[part : 2 * part].astype(BF)
        kv[s, 1] = (qkv[2 * part :] + bias_col[part:]).astype(BF)
        kv_copy(s).start()

    def kvg_copy(s):
        return remote(kvs.at[s], kvg.at[s], pair(s_kvg, s), dev_core)

    def finish(s):
        kvg_copy(s).wait_recv()
        dq = qt[s]
        dkv = (kv[s].astype(F32) + kvg[s].astype(F32)).astype(BF).reshape(2 * part, half)
        ones = jnp.ones((8, half), BF)
        sums[s, 1:2, :part] = dot(ones, dq, NT)[:1]
        sums[s, 1:2, part : 2 * part] = dot(ones, dkv[part:], NT)[:1]
        sums[s, 1:2, 2 * part :] = jnp.zeros((1, width - 2 * part), F32)
        stacked = jnp.concatenate([dq, dkv], axis=0)
        acc[...] += dot(stacked, att_weights(s)[: 3 * part], TN)
        w_att[s, 0:3] = dot(stacked, n1[...], NN).astype(BF).reshape(3, 2, 96, width)
        fold_1(ATT, s)

    def sums_copy(s):
        return remote(
            sums.at[s],
            sums_z.at[t],
            (s_sz.at[0, s], s_sz.at[1, t]),
            at(d, source[s]),
        )

    def sums_got(s):
        ref = sums_z.at[source[s]]
        remote(ref, ref, (s_sz.at[0, s], s_sz.at[1, source[s]]), dev_core).wait_recv()

    dev_x = at(base + 2 * yx_x + c, t)
    dev_y = at(base + 2 * yx_y + c, t)

    def flip(k):
        return remote(
            sums_p.at[2 * k], sums_p.at[2 * k + 1], pair(s_sp, k), (dev_core, dev_x, dev_y)[k]
        )

    def sums_start():
        for s in range(1, lines):
            sums_copy(s).start()
        sums_z[pl.ds(t, 1)] = sums[0:1]

    def sums_line():
        for s in range(1, lines):
            sums_got(s)
        sums_p[0] = (sums_z[0] + sums_z[1]) + (sums_z[2] + sums_z[3])
        flip(0).start()

    def sums_plane(k):
        flip(k - 1).wait()
        sums_p[2 * k] = sums_p[2 * k - 2] + sums_p[2 * k - 1]
        flip(k).start()

    def sums_end():
        flip(2).wait()
        small_out[...] = sums_p[4] + sums_p[5]

    steps = {
        Z_OWN: z_own,
        Z_PASS: z_pass,
        STEP_1: step_1,
        STEP_2: step_2,
        STEP_3: step_3,
        FOLD_2: fold_2,
        FOLD_3: fold_3,
        FOLD_4: fold_4,
        FOLD_5: fold_5,
        TOTAL: total,
        SPREAD_2: spread_step_2,
        SPREAD_3: spread_step_3,
        FINISH: finish,
        SEE: see,
        SUMS: sums_start,
        SUMS_Z: sums_line,
        SUMS_P: sums_plane,
        SUMS_END: sums_end,
        MOVE: lambda name, *which: to_owner(*rows[name], *which),
    }
    rows = {
        X: (tokens, xb, s_x),
        G: (cotangent, gb, s_g),
        BO: (bo, block_home, s_bo),
        IG: (ig, input_home, s_ig),
    }

    def run(*where):
        for name, *which in PLAN.get(where, ()):
            steps[name](*which)

    def point(loop, j, where):
        for k in range(lines):
            if (loop, k, where) in PLAN:
                pl.when(j == k)(functools.partial(run, loop, k, where))

    run(START)
    to_owner_wait(tokens, xb, s_x)
    run(X_HERE)
    normed, _ = norm_parts(xb[...].reshape(half, width).astype(F32))
    n1[...] = (normed * gain_first + shift_first).astype(BF)
    for s in range(1, lines):
        bias_got(s)
    project(0)
    run(FIRST)

    def attend(s, carry):
        @pl.when(s < lines - 1)
        def _():
            step_4(ATT, s + 1)
            project(s + 1)

        kv_copy(s).wait_recv()
        for h in range(part // HEAD):
            rows = slice(h * HEAD, (h + 1) * HEAD)
            q = qt[s, rows, :]
            s0 = dot(kv[s, 0, rows, :].T, q, NN) * FACTOR + mask[0]
            s1 = dot(kvs[s, 0, rows, :].T, q, NN) * FACTOR + mask[1]
            top = jnp.maximum(
                jnp.max(s0, axis=0, keepdims=True), jnp.max(s1, axis=0, keepdims=True)
            )
            p0 = jnp.exp2(s0 - top)
            p1 = jnp.exp2(s1 - top)
            weight = column_sum(p0) + column_sum(p1)
            out = dot(kv[s, 1, rows, :], p0.astype(BF), NN)
            out = out + dot(kvs[s, 1, rows, :], p1.astype(BF), NN)
            ct[s, rows, :] = (out / weight).astype(BF)
            lse[s, h : h + 1, :] = top + jnp.log2(weight)
            point(ATTEND, s, h)
        return carry

    lax.fori_loop(0, lines, attend, 0)

    mid = xb[...].reshape(half, width).astype(F32) + bias_out
    for s in range(lines):
        mid = mid + dot(ct[s], att_weights(s)[3 * part :], TN)
    middle[...] = mid
    normed, _ = norm_parts(mid)
    low_normed = (normed * gain_second + shift_second).astype(BF)
    n2[...] = low_normed
    n2t[...] = low_normed.T
    acc[...] = jnp.zeros_like(acc)
    acc2[...] = jnp.zeros_like(acc2)
    run(OUT)
    to_owner_wait(cotangent, gb, s_g)

    def feed(s, carry):
        @pl.when(s > 0)
        def _():
            step_4(FFN, s)

        for k in range(lines):
            pl.when(s == k)(functools.partial(z_sent, FFN, k))
        point(FEED, s, 0)
        grad = gb[...].reshape(half, width)
        pre = dot(n2[...], up_weights(s), NN) + bias[s, 0:1, :]
        phi = 0.5 * (1.0 + lax.erf(pre * 0.7071067811865476))
        active = (pre * phi).astype(BF)
        slope = phi + pre * jnp.exp(-0.5 * pre * pre) * 0.3989422804014327
        acc[...] += dot(active, down_weights(s), NN)
        point(FEED, s, 1)
        pre_grad = (dot(grad, down_weights(s), NT) * slope).astype(BF)
        sums[s, 0:1, :] = column_sum(pre_grad.astype(F32))
        point(FEED, s, 2)
        acc2[...] += dot(pre_grad, up_weights(s), NT)
        point(FEED, s, 3)
        w_ffn[s, :, :, 1] = dot(active, grad, TN).astype(BF).reshape(4, 2, 96, width)
        point(FEED, s, 4)
        w_ffn[s, :, :, 0] = dot(n2t[...], pre_grad, NN).astype(BF).reshape(4, 2, 96, width)
        fold_1(FFN, s)
        point(FEED, s, 5)
        return carry

    lax.fori_loop(0, lines, feed, 0)

    mid = middle[...]
    bo[...] = (mid + acc[...] + bias_down).astype(BF).reshape(2, 256, width)
    run(BLOCK)
    normed, rate = norm_parts(mid)
    grad = gb[...].reshape(half, width).astype(F32)
    back = acc2[...]
    middle_grad = grad + norm_back(normed, rate, back, gain_second)
    vec_out = column_sum(middle_grad)
    vec_gain = column_sum(back * normed)
    vec_shift = column_sum(back)
    vec_down = column_sum(grad)
    for s in range(lines):
        sums[s, 4:5, :] = vec_out
        sums[s, 5:6, :] = vec_gain
        sums[s, 6:7, :] = vec_shift
        sums[s, 7:8, :] = vec_down
    acc2[...] = middle_grad
    dmr[...] = middle_grad.astype(BF)
    acc[...] = jnp.zeros_like(acc)
    for s in range(lines):
        z_sent(ATT, s)
    run(NORM)

    def attend_back(j, carry):
        s = by_line_of(j, *ORDER)
        dct = dot(w_att[s, 3].reshape(part, width), dmr[...], NT).astype(BF)
        w_att[s, 3] = dot(ct[s], dmr[...], NN).astype(BF).reshape(2, 96, width)
        kv_copy(s).wait_send()
        point(BACK, j, 0)
        for h in range(part // HEAD):
            rows = slice(h * HEAD, (h + 1) * HEAD)
            g = dct[rows]
            q = qt[s, rows, :]
            along = column_sum(g.astype(F32) * ct[s, rows, :].astype(F32))
            total_log = lse[s, h : h + 1, :]
            dq = jnp.zeros((HEAD, half), F32)
            for place, ref in enumerate((kv, kvs)):
                k = ref[s, 0, rows, :]
                v = ref[s, 1, rows, :]
                p = jnp.exp2(dot(k.T, q, NN) * FACTOR + mask[place] - total_log)
                ds = (p * (dot(v.T, g, NN) - along)).astype(BF)
                ref[s, 0, rows, :] = (dot(q, ds, NT) * HEAD**-0.5).astype(BF)
                ref[s, 1, rows, :] = dot(g, p.astype(BF), NT).astype(BF)
                dq = dq + dot(k, ds, NN)
            qt[s, rows, :] = (dq * HEAD**-0.5).astype(BF)
            if h == part // HEAD - 1:
                kvg_copy(s).start()
            point(BACK, j, h + 1)
        return carry

    lax.fori_loop(0, lines, attend_back, 0)
    run(TAIL_0)

    normed, rate = norm_parts(xb[...].reshape(half, width).astype(F32))
    back = acc[...]
    vec_gain = column_sum(back * normed)
    vec_shift = column_sum(back)
    for s in range(lines):
        sums[s, 2:3, :] = vec_gain
        sums[s, 3:4, :] = vec_shift

    run(TAIL_1)
    ig[...] = (
        (acc2[...] + norm_back(normed, rate, back, gain_first))
        .astype(BF)
        .reshape(2, 256, width)
    )
    run(TAIL_2)
    run(TAIL_3)

    ids_copy.wait_send()
    for s in range(1, lines):
        bias_copy(s).wait_send()
        sums_copy(s).wait_send()
    to_owner_sent(tokens, s_x)
    to_owner_sent(cotangent, s_g)
    to_owner_wait(bo, block_home, s_bo)
    to_owner_sent(bo, s_bo)
    for s in range(lines):
        kvg_copy(s).wait_send()
    for i in (ATT, FFN):
        for s in range(lines):
            reduce_core(i, s).wait_send()
            reduce_a(i, s, 0).wait_send()
            reduce_a(i, s, 1).wait_send()
            reduce_b(i, s).wait_send()
            if s > 0:
                reduce_z(i, s).wait_send()
        for m in range(1 + i if whole_plane else 0):
            spread_1(i, m).wait_send()
            spread_2(i, m, 0).wait_send()
            spread_2(i, m, 1).wait_send()
            spread_3(i, m).wait()
    to_owner_wait(ig, input_home, s_ig)
    to_owner_sent(ig, s_ig)


def layer(lines, whole_plane, operands):
    def dma(*shape):
        return pltpu.SemaphoreType.DMA((2,) + shape)

    def vmem(*shape, dtype=BF):
        return pltpu.VMEM(shape, dtype)

    n = lines
    anywhere = pl.BlockSpec(memory_space=pl.ANY)
    inside = pl.BlockSpec(memory_space=pltpu.VMEM)
    att = (96, 768)
    ffn = (2, 96, 768)
    plane = (4, 2) if whole_plane else ()
    blocks = jax.ShapeDtypeStruct((2, 256, 768), BF)
    return pl.pallas_call(
        functools.partial(layer_kernel, lines, whole_plane),
        in_specs=[anywhere, anywhere, inside] + [anywhere] * 4 + [inside] * 8,
        out_specs=[anywhere] * 5 + [inside],
        out_shape=[
            blocks,
            blocks,
            jax.ShapeDtypeStruct(plane + att, BF),
            jax.ShapeDtypeStruct(plane + att, BF),
            jax.ShapeDtypeStruct(plane + att, BF),
            jax.ShapeDtypeStruct((8, 768), F32),
        ],
        scratch_shapes=[
            vmem(n, 4, 2, *att),
            vmem(n, 4, 2, *ffn),
            vmem(n, 4, *att),
            vmem(n, 4, *ffn),
            vmem(n, 2, *att),
            vmem(n, 2, *ffn),
            vmem(n, *att),
            vmem(n, *ffn),
            vmem(5, *att),
            vmem(5, *ffn),
            vmem(2, 256, 768),
            vmem(2, 256, 768),
            vmem(2, 2, 1024, dtype=jnp.int32),
            vmem(n, 8, 768, dtype=F32),
            vmem(2, 512, 512, dtype=F32),
            vmem(512, 768),
            vmem(512, 768),
            vmem(768, 512),
            vmem(512, 768, dtype=F32),
            vmem(512, 768, dtype=F32),
            vmem(512, 768, dtype=F32),
            vmem(512, 768),
            vmem(n, 192, 512),
            vmem(n, 2, 192, 512),
            vmem(n, 2, 192, 512),
            vmem(n, 2, 192, 512),
            vmem(n, 192, 512),
            vmem(n, 8, 512, dtype=F32),
            vmem(2, 256, 768),
            vmem(2, 256, 768),
            vmem(n, 8, 768, dtype=F32),
            vmem(n, 8, 768, dtype=F32),
            vmem(6, 8, 768, dtype=F32),
            pltpu.SemaphoreType.DMA((7,)),
            dma(),
            dma(n),
            dma(2, 2),
            dma(2, 2),
            dma(2, 2),
            dma(2, 2),
            dma(n),
            dma(n),
            pltpu.SemaphoreType.DMA((2, 5)),
            pltpu.SemaphoreType.DMA((2, n)),
            dma(2, n - 1),
            dma(2, n - 1, 2),
            dma(2, n - 1),
            dma(2, n),
            dma(2, n, 2),
            dma(2, n),
            pltpu.SemaphoreType.DMA((2, n)),
            pltpu.SemaphoreType.DMA((2, 5)),
            dma(3),
            dma(3, 2),
            dma(3),
            dma(n),
            dma(3),
        ],
        compiler_params=pltpu.CompilerParams(
            collective_id=0, has_side_effects=True, vmem_limit_bytes=62 * 2**20
        ),
        name="layer",
    )(*operands)


def results_kernel(
    block_in, input_in, att_in, up_in, down_in, small_in,
    block_out, input_out, qkv_out, out_out, up_out, down_out, bias_out, *rest
):
    sums_out, (low_in, low_att, low_up, low_down) = rest[:7], rest[7:11]
    wide_in, wide_att, wide_up, wide_down, low_block, s_in, s_out, s_block = rest[11:]
    part = bias_out.shape[1]
    third = 3 * part
    block = pltpu.make_async_copy(block_in, low_block, s_block)
    jobs = [(up_in, low_up, wide_up, up_out, 0, 0, 2 * part)]
    jobs += [(up_in, low_up, wide_up, up_out, 2 * part, 2 * part, 2 * part)]
    jobs += [(down_in, low_down, wide_down, down_out, k, k, 2 * part) for k in (0, 2 * part)]
    jobs += [(att_in, low_att, wide_att, qkv_out, 0, 0, third)]
    jobs += [(att_in, low_att, wide_att, out_out, third, 0, part)]
    jobs += [(input_in, low_in, wide_in, input_out, k, k, 256) for k in (0, 256)]

    def fetch(k):
        source, low, _, _, at, _, size = jobs[k]
        rows = pl.ds(at, size)
        return pltpu.make_async_copy(source.at[rows], low.at[rows], s_in.at[k])

    def store(k):
        _, _, wide, result, at, to, size = jobs[k]
        return pltpu.make_async_copy(wide.at[pl.ds(at, size)], result.at[pl.ds(to, size)], s_out.at[k])

    for k in range(len(jobs)):
        fetch(k).start()
    block.start()
    bias_out[0:1] = small_in[1:2, :part]
    bias_out[1:2] = small_in[1:2, part : 2 * part]
    for ref, row in zip(sums_out, (0, 2, 3, 4, 5, 6, 7)):
        ref[...] = small_in[row]
    for k, (_, low, wide, _, at, _, size) in enumerate(jobs):
        fetch(k).wait()
        wide[pl.ds(at, size)] = low[pl.ds(at, size)].astype(F32)
        store(k).start()
    block.wait()
    block = pltpu.make_async_copy(low_block, block_out, s_block)
    block.start()
    for k in range(len(jobs)):
        store(k).wait()
    block.wait()


def results(block, inputs, att, up, down, small):
    width = att.shape[0]
    part = width // 4
    tokens = inputs.shape[0] * inputs.shape[1]
    anywhere = pl.BlockSpec(memory_space=pl.ANY)
    inside = pl.BlockSpec(memory_space=pltpu.VMEM)
    shapes = ((tokens, width), (width, width), (width, width), (width, width))
    block, inputs, *results = pl.pallas_call(
        results_kernel,
        in_specs=[anywhere] * 5 + [inside],
        out_specs=[anywhere] * 6 + [inside] * 8,
        out_shape=[
            jax.ShapeDtypeStruct(block.shape, BF),
            jax.ShapeDtypeStruct((tokens, width), F32),
            jax.ShapeDtypeStruct((3 * part, width), F32),
            jax.ShapeDtypeStruct((part, width), F32),
            jax.ShapeDtypeStruct((width, width), F32),
            jax.ShapeDtypeStruct((width, width), F32),
            jax.ShapeDtypeStruct((2, part), F32),
        ]
        + [jax.ShapeDtypeStruct((width,), F32)] * 7,
        scratch_shapes=[pltpu.VMEM(shape, BF) for shape in shapes]
        + [pltpu.VMEM(shape, F32) for shape in shapes]
        + [pltpu.VMEM(block.shape, BF)]
        + [pltpu.SemaphoreType.DMA((8,)), pltpu.SemaphoreType.DMA((8,)), pltpu.SemaphoreType.DMA],
        compiler_params=pltpu.CompilerParams(vmem_limit_bytes=62 * 2**20),
        name="results",
    )(block, inputs.reshape(tokens, width), att, up, down, small)
    return (block, inputs.reshape(block.shape), *results)


def body(
    dp,
    lines,
    tokens,
    segment_ids,
    gain_first,
    shift_first,
    weight_qkv,
    bias_qv,
    weight_out,
    bias_out,
    gain_second,
    shift_second,
    weight_up,
    bias_up,
    weight_down,
    bias_down,
    cotangent,
):
    width = tokens.shape[2]
    part = weight_qkv.shape[2]
    shard = (4, 2, width // PLANE, width)
    whole_plane = dp == PLANE
    block_out, input_grad, *grads, small = layer(
        lines,
        whole_plane,
        (
            tokens,
            cotangent,
            segment_ids,
            weight_qkv.reshape(width, 3 * part).T.reshape(3, 2, width // PLANE, width),
            weight_out.reshape(2, width // PLANE, width),
            weight_up.reshape(shard),
            weight_down.reshape(shard),
            bias_up,
            bias_qv,
            gain_first,
            shift_first,
            bias_out,
            gain_second,
            shift_second,
            bias_down,
        ),
    )
    if not whole_plane:
        apart = [[i + PLANE * g for g in range(dp // PLANE)] for i in range(PLANE)]
        planes = [[i + PLANE * g for i in range(PLANE)] for g in range(dp // PLANE)]
        sums = tuple(grad.astype(F32) for grad in grads)
        *grads, small = lax.psum(sums + (small,), "dp", axis_index_groups=apart)
        grads = [lax.all_gather(g.astype(BF), "dp", axis_index_groups=planes) for g in grads]
    att_grad, up_grad, down_grad = [grad.reshape(width, width) for grad in grads]
    block_out, input_grad, qkv_grad, out_grad, up_grad, down_grad, bias_grad, *sums = results(
        block_out, input_grad, att_grad, up_grad, down_grad, small
    )
    up_bias, gain_one, shift_one, out_bias, gain_two, shift_two, down_bias = sums
    return (
        block_out,
        input_grad,
        gain_one,
        shift_one,
        qkv_grad.T.reshape(width, 3, part),
        bias_grad,
        out_grad,
        out_bias,
        gain_two,
        shift_two,
        up_grad,
        up_bias,
        down_grad,
        down_bias,
    )


def solution(mesh):
    in_specs = (
        P("dp", "tensor", None),
        P("dp", None),
        P(),
        P(),
        P(None, None, "tensor"),
        P(None, "tensor"),
        P("tensor", None),
        P(),
        P(),
        P(),
        P(None, "tensor"),
        P("tensor"),
        P("tensor", None),
        P(),
        P("dp", "tensor", None),
    )
    out_specs = (
        P("dp", "tensor", None),
        P("dp", "tensor", None),
        P(),
        P(),
        P(None, None, "tensor"),
        P(None, "tensor"),
        P("tensor", None),
        P(),
        P(),
        P(),
        P(None, "tensor"),
        P("tensor"),
        P("tensor", None),
        P(),
    )
    whole = functools.partial(body, mesh.shape["dp"], mesh.shape["tensor"])
    return jax.shard_map(whole, mesh=mesh, in_specs=in_specs, out_specs=out_specs, check_vma=False)
```

```python
import functools

import jax
import jax.numpy as jnp
from jax import lax
from jax.experimental import pallas as pl
from jax.experimental.pallas import tpu as pltpu
from jax.sharding import PartitionSpec as P

HEAD = 64
PLANE = 8
FACTOR = HEAD**-0.5 * 1.4426950408889634
BF = jnp.bfloat16
F32 = jnp.float32
NN = ((1,), (0,))
NT = ((1,), (1,))
TN = ((0,), (0,))
ATT, FFN = 0, 1

Z_OWN, Z_PASS, STEP_1, STEP_2, STEP_3, FOLD_2, FOLD_3, FOLD_4, FOLD_5, TOTAL = range(10)
SPREAD_2, SPREAD_3, FINISH, SEE, SUMS, SUMS_Z, SUMS_P, SUMS_END, MOVE = range(10, 19)
X, G, BO, IG = range(4)
START, X_HERE, FIRST, ATTEND, OUT, FEED, BLOCK, NORM, BACK, TAIL_0, TAIL_1, TAIL_2, TAIL_3 = range(13)

ORDER = (3, 2, 1, 0)

PLAN = {
    (START,): (
        (Z_OWN, ATT),
        (MOVE, X, 0, 0),
        (MOVE, X, 1, 1),
        (Z_PASS, ATT, 1),
        (Z_PASS, ATT, 2),
        (STEP_1, ATT, 1),
        (Z_OWN, FFN),
        (STEP_1, ATT, 2),
        (STEP_2, ATT, 1),
        (Z_PASS, ATT, 3),
        (MOVE, X, 0, 1),
        (MOVE, X, 1, 0),
        (STEP_1, ATT, 3),
        (SEE,),
        (Z_PASS, FFN, 1),
        (STEP_1, FFN, 1),
        (STEP_2, ATT, 2),
    ),
    (X_HERE,): (
        (MOVE, G, 0, 0),
        (Z_PASS, FFN, 2),
        (STEP_3, ATT, 1),
        (STEP_2, ATT, 3),
    ),
    (FIRST,): (
        (STEP_3, ATT, 2),
        (STEP_1, FFN, 2),
    ),
    (ATTEND, 0, 0): (
        (STEP_2, FFN, 1),
        (MOVE, G, 1, 0),
    ),
    (ATTEND, 1, 0): (
        (Z_PASS, FFN, 3),
        (MOVE, G, 1, 1),
    ),
    (ATTEND, 1, 2): (
        (STEP_3, ATT, 3),
        (STEP_2, FFN, 2),
        (MOVE, G, 0, 1),
    ),
    (ATTEND, 2, 2): (
        (STEP_3, FFN, 1),
    ),
    (ATTEND, 3, 2): (
        (STEP_1, FFN, 3),
    ),
    (FEED, 0, 3): (
        (STEP_3, FFN, 2),
        (STEP_2, FFN, 3),
    ),
    (FEED, 2, 1): (
        (FOLD_2, FFN, 0),
        (STEP_3, FFN, 3),
    ),
    (FEED, 2, 3): (
        (FOLD_2, FFN, 1),
    ),
    (BLOCK,): (
        (MOVE, BO, 1, 1),
    ),
    (BACK, 0, 1): (
        (FOLD_2, FFN, 3),
    ),
    (BACK, 0, 3): (
        (MOVE, BO, 1, 0),
    ),
    (BACK, 1, 0): (
        (MOVE, BO, 0, 0),
        (FOLD_2, FFN, 2),
    ),
    (BACK, 1, 1): (
        (FINISH, 3),
        (FOLD_3, FFN, 3),
    ),
    (BACK, 1, 2): (
        (FOLD_2, ATT, 3),
    ),
    (BACK, 1, 3): (
        (MOVE, BO, 0, 1),
        (FINISH, 2),
    ),
    (BACK, 2, 0): (
        (FOLD_4, FFN, 3),
    ),
    (BACK, 2, 1): (
        (FOLD_3, FFN, 2),
    ),
    (BACK, 3, 0): (
        (FOLD_3, ATT, 3),
        (FOLD_3, FFN, 1),
    ),
    (BACK, 3, 1): (
        (FOLD_4, FFN, 2),
        (FOLD_5, FFN, 3),
        (FOLD_2, ATT, 2),
    ),
    (BACK, 3, 2): (
        (FINISH, 1),
        (FOLD_3, FFN, 0),
    ),
    (BACK, 3, 3): (
        (FOLD_4, ATT, 3),
        (FOLD_4, FFN, 1),
        (FOLD_2, ATT, 1),
        (FOLD_5, FFN, 2),
        (FOLD_5, FFN, 1),
    ),
    (TAIL_0,): (
        (FINISH, 0),
        (FOLD_3, ATT, 2),
    ),
    (TAIL_1,): (
        (FOLD_2, ATT, 0),
        (FOLD_5, ATT, 3),
        (FOLD_3, ATT, 1),
    ),
    (TAIL_2,): (
        (FOLD_4, FFN, 0),
        (FOLD_4, ATT, 2),
        (SUMS,),
        (MOVE, IG, 1, 0),
        (TOTAL, FFN),
        (FOLD_3, ATT, 0),
        (FOLD_4, ATT, 1),
        (FOLD_5, ATT, 2),
        (SUMS_Z,),
        (MOVE, IG, 0, 1),
    ),
    (TAIL_3,): (
        (FOLD_4, ATT, 0),
        (FOLD_5, ATT, 1),
        (SUMS_P, 1),
        (SPREAD_2, FFN),
        (MOVE, IG, 1, 1),
        (TOTAL, ATT),
        (MOVE, IG, 0, 0),
        (SPREAD_2, ATT),
        (SUMS_P, 2),
        (SPREAD_3, FFN),
        (SPREAD_3, ATT),
        (SUMS_END,),
    ),
}


def dot(left, right, dims):
    return lax.dot_general(left, right, (dims, ((), ())), preferred_element_type=F32)


def norm_parts(values):
    center = values - jnp.mean(values, axis=-1, keepdims=True)
    rate = lax.rsqrt(jnp.mean(center * center, axis=-1, keepdims=True) + 1e-5)
    return center * rate, rate


def norm_back(normed, rate, grad, gain):
    scaled = grad * gain
    mean = jnp.mean(scaled, axis=-1, keepdims=True)
    along = jnp.mean(scaled * normed, axis=-1, keepdims=True)
    return rate * (scaled - mean - normed * along)


def column_sum(values):
    return jnp.sum(values, axis=0, keepdims=True)


def layer_kernel(
    lines,
    whole_plane,
    tokens,
    cotangent,
    ids_in,
    shard_qkv,
    shard_out,
    shard_up,
    shard_down,
    bias_up,
    bias_qv,
    gain_first,
    shift_first,
    bias_out,
    gain_second,
    shift_second,
    bias_down,
    block_home,
    input_home,
    grads_att,
    grads_up,
    grads_down,
    small_out,
    w_att,
    w_ffn,
    r_core_att,
    r_core_ffn,
    r_a_att,
    r_a_ffn,
    r_b_att,
    r_b_ffn,
    r_z_att,
    r_z_ffn,
    xb,
    gb,
    ids,
    bias,
    mask,
    n1,
    n2,
    n2t,
    middle,
    acc,
    acc2,
    dmr,
    qt,
    kv,
    kvs,
    kvg,
    ct,
    lse,
    bo,
    ig,
    sums,
    sums_z,
    sums_p,
    s_loc,
    s_ids,
    s_bias,
    s_x,
    s_g,
    s_bo,
    s_ig,
    s_kv,
    s_kvg,
    s_zs,
    s_zr,
    s_1,
    s_2,
    s_3,
    s_c,
    s_a,
    s_b,
    s_zgs,
    s_zgr,
    s_g1,
    s_g2,
    s_g3,
    s_sz,
    s_sp,
):
    t = lax.axis_index("tensor")
    d = lax.axis_index("dp")
    e = lax.rem(d, PLANE)
    base = d - e
    c = lax.rem(e, 2)
    yx = e // 2
    x_bit = lax.rem(yx, 2)
    y_bit = yx // 2
    half = 512
    part = 192
    width = 768
    w_of = (w_att, w_ffn)
    r_core = (r_core_att, r_core_ffn)
    r_a = (r_a_att, r_a_ffn)
    r_b = (r_b_att, r_b_ffn)
    r_z = (r_z_att, r_z_ffn)
    grads_out = ((grads_att,), (grads_up, grads_down))
    gain_first, shift_first, bias_out = [r[...][None] for r in (gain_first, shift_first, bias_out)]
    gain_second, shift_second = gain_second[...][None], shift_second[...][None]
    bias_down = bias_down[...][None]

    yx_x = 2 * y_bit + 1 - x_bit
    yx_y = 2 * (1 - y_bit) + x_bit
    yx_first = (1 - c) * yx_x + c * yx_y
    yx_second = (1 - c) * yx_y + c * yx_x

    def at(dp_index, line):
        return {"dp": dp_index, "tensor": line}

    dev_core = at(base + 2 * yx + 1 - c, t)
    dev_first = at(base + 2 * yx_first + c, t)
    dev_second = at(base + 2 * yx_second + c, t)

    def by_line_of(place, *values):
        out = values[3]
        for k in (2, 1, 0):
            out = jnp.where(place == k, values[k], out)
        return out

    def by_line(*values):
        return by_line_of(t, *values)

    source = [t, by_line(1, 2, 3, 2), by_line(2, 0, 1, 1), by_line(3, 3, 0, 0)]
    inner = jnp.logical_and(t > 0, t < lines - 1)
    outer = jnp.logical_not(inner)

    def remote(src, dst, sems, dev):
        return pltpu.make_async_remote_copy(
            src_ref=src,
            dst_ref=dst,
            send_sem=sems[0],
            recv_sem=sems[1],
            device_id=dev,
            device_id_type=pl.DeviceIdType.MESH,
        )

    def pair(sem, *index):
        return sem.at[(0,) + index], sem.at[(1,) + index]

    barrier = pltpu.get_barrier_semaphore()
    for step in range(lines):
        for core in range(2):
            if step == 0 and core == 0:
                continue
            other = base + 2 * yx + lax.rem(c + core, 2)
            pl.semaphore_signal(
                barrier,
                1,
                device_id=at(other, lax.rem(t + step, lines)),
                device_id_type=pl.DeviceIdType.MESH,
            )
    for dev in (dev_first, dev_second):
        pl.semaphore_signal(barrier, 1, device_id=dev, device_id_type=pl.DeviceIdType.MESH)
    pl.semaphore_wait(barrier, 2 * lines - 1 + 2)

    def to_owner(src, dst, sem, m, h):
        here = jnp.logical_and(t == 2 * c + m, c == t // 2)
        place = lax.rem(t, 2)
        dev = at(base + 2 * yx + t // 2, 2 * c + m)
        rows = pl.ds(128 * h, 128)
        out, into = src.at[m, rows], dst.at[place, rows]

        @pl.when(here)
        def _():
            pltpu.make_async_copy(out, into, sem.at[1, place, h]).start()

        @pl.when(jnp.logical_not(here))
        def _():
            remote(out, into, (sem.at[0, m, h], sem.at[1, place, h]), dev).start()

    def to_owner_wait(src, dst, sem):
        for k in range(2):
            for h in range(2):
                ref = dst.at[k, pl.ds(128 * h, 128)]
                pltpu.make_async_copy(ref, ref, sem.at[1, k, h]).wait()

    def to_owner_sent(src, sem):
        for m in range(2):
            here = jnp.logical_and(t == 2 * c + m, c == t // 2)

            @pl.when(jnp.logical_not(here))
            def _():
                for h in range(2):
                    ref = src.at[m, pl.ds(128 * h, 128)]
                    remote(ref, ref, (sem.at[0, m, h], sem.at[1, m, h]), dev_core).wait_send()

    def piece(i, s, place):
        return w_of[i].at[s, place, c]

    def z_right(i, src):
        slot = 2 - t // 2
        return remote(
            src, w_of[i].at[slot, yx, c], (s_zs.at[i, 0], s_zr.at[i, slot]), at(d, t + 1)
        )

    def z_left(i, src):
        return remote(src, w_of[i].at[1, yx, c], (s_zs.at[i, 1], s_zr.at[i, 1]), at(d, t - 1))

    def z_own(i):
        for copy in own[2 * i : 2 * i + 2]:
            copy.wait()
        pl.when(t < lines - 1)(lambda: z_right(i, own_piece[i]).start())
        pl.when(t > 0)(lambda: z_left(i, own_piece[i]).start())

    def z_forward(i, s):
        slot = (0, t + 1, 4 - t, 3)[s]
        line = (0, t - 1, t + 1, 3 * t - 3)[s]
        src = piece(i, s, yx)
        return remote(
            src, w_of[i].at[slot, yx, c], (s_zs.at[i, 1 + s], s_zr.at[i, slot]), at(d, line)
        )

    def z_got(i, s):
        ref = piece(i, s, yx)
        remote(ref, ref, (s_zs.at[i, 1 + s], s_zr.at[i, s]), dev_core).wait_recv()

    def z_pass(i, s):
        @pl.when(inner)
        def _():
            z_got(i, s)
            z_forward(i, s).start()

    def z_sent(i, s):
        if s == 0:
            pl.when(t < lines - 1)(lambda: z_right(i, own_piece[i]).wait_send())
            pl.when(t > 0)(lambda: z_left(i, own_piece[i]).wait_send())
        else:
            pl.when(inner)(lambda: z_forward(i, s).wait_send())

    def gather_1(i, s):
        ref = piece(i, s, yx)
        return remote(ref, ref, pair(s_1, i, s - 1), dev_first)

    def gather_2(i, s, k):
        ref = piece(i, s, yx if k == 0 else yx_first)
        return remote(ref, ref, pair(s_2, i, s - 1, k), dev_second)

    def gather_3(i, s):
        ref = w_of[i].at[s, :, c]
        return remote(ref, ref, pair(s_3, i, s - 1), dev_core)

    def step_1(i, s):
        pl.when(outer)(lambda: z_got(i, s))
        gather_1(i, s).start()

    def step_2(i, s):
        gather_1(i, s).wait_recv()
        gather_2(i, s, 0).start()
        gather_2(i, s, 1).start()

    def step_3(i, s):
        gather_2(i, s, 0).wait_recv()
        gather_2(i, s, 1).wait_recv()
        gather_3(i, s).start()

    def step_4(i, s):
        gather_3(i, s).wait()
        gather_1(i, s).wait_send()
        gather_2(i, s, 0).wait_send()
        gather_2(i, s, 1).wait_send()

    def add_into(dst, src):
        dst[...] = dst[...] + src[...]

    send_k = [(1 - c) * (2 * k + 1 - x_bit) + c * (2 * (1 - y_bit) + k) for k in range(2)]
    keep_k = [(1 - c) * (2 * k + x_bit) + c * (2 * y_bit + k) for k in range(2)]
    k_mine = (1 - c) * y_bit + c * x_bit

    def reduce_core(i, s):
        return remote(w_of[i].at[s, :, 1 - c], r_core[i].at[s], pair(s_c, i, s), dev_core)

    def reduce_a(i, s, k):
        return remote(piece(i, s, send_k[k]), r_a[i].at[s, k], pair(s_a, i, s, k), dev_first)

    def reduce_b(i, s):
        return remote(piece(i, s, yx_second), r_b[i].at[s], pair(s_b, i, s), dev_second)

    def reduce_z(i, s):
        line = (0, by_line(1, 2, 3, 2), by_line(1, 0, 1, 2), by_line(1, 2, 1, 2))[s]
        place = (0, by_line(3, 3, 3, 4), by_line(0, 4, 4, 1), by_line(2, 0, 1, 2))[s]
        return remote(
            piece(i, s, yx), r_z[i].at[place], (s_zgs.at[i, s], s_zgr.at[i, place]), at(d, line)
        )

    def reduce_z_got(i, place):
        ref = r_z[i].at[place]
        remote(ref, ref, (s_zgs.at[i, 1], s_zgr.at[i, place]), dev_core).wait_recv()

    def fold_1(i, s):
        reduce_core(i, s).start()

    def fold_2(i, s):
        reduce_core(i, s).wait_recv()
        for k in range(2):
            add_into(piece(i, s, send_k[k]), r_core[i].at[s, send_k[k]])
            reduce_a(i, s, k).start()
        for k in range(2):
            add_into(piece(i, s, keep_k[k]), r_core[i].at[s, keep_k[k]])

    def fold_3(i, s):
        reduce_a(i, s, 0).wait_recv()
        reduce_a(i, s, 1).wait_recv()
        add_into(piece(i, s, yx_second), r_a[i].at[s, 1 - k_mine])
        reduce_b(i, s).start()
        add_into(piece(i, s, yx), r_a[i].at[s, k_mine])

    def fold_4(i, s):
        reduce_b(i, s).wait_recv()
        add_into(piece(i, s, yx), r_b[i].at[s])
        if s > 0:
            pl.when(outer)(lambda: reduce_z(i, s).start())

    def fold_5(i, s):
        @pl.when(inner)
        def _():
            reduce_z_got(i, s - 1)
            add_into(piece(i, s, yx), r_z[i].at[s - 1])
            reduce_z(i, s).start()

    def own_total(i, m):
        ref = piece(i, 0, yx)
        return ref if i == ATT else ref.at[m]

    def spread_1(i, m):
        dst = grads_out[i][m].at[yx, c]
        return remote(own_total(i, m), dst, pair(s_g1, i + m), dev_first)

    def spread_2(i, m, k):
        if k == 0:
            dst = grads_out[i][m].at[yx, c]
            return remote(own_total(i, m), dst, pair(s_g2, i + m, 0), dev_second)
        ref = grads_out[i][m].at[yx_first, c]
        return remote(ref, ref, pair(s_g2, i + m, 1), dev_second)

    def spread_3(i, m):
        ref = grads_out[i][m].at[:, c]
        return remote(ref, ref, pair(s_g3, i + m), dev_core)

    def keep_total(i, m):
        dst = grads_out[i][m].at[yx, c] if whole_plane else grads_out[i][m]
        return pltpu.make_async_copy(own_total(i, m), dst, s_loc.at[4 + i + m])

    def total(i):
        for side, there in ((3, t > 0), (4, t < lines - 1)):

            @pl.when(there)
            def _():
                reduce_z_got(i, side)
                add_into(piece(i, 0, yx), r_z[i].at[side])

        for m in range(1 + i):
            keep_total(i, m).start()
            if whole_plane:
                spread_1(i, m).start()

    def spread_step_2(i):
        if whole_plane:
            for m in range(1 + i):
                spread_2(i, m, 0).start()
            for m in range(1 + i):
                spread_1(i, m).wait_recv()
                spread_2(i, m, 1).start()

    def spread_step_3(i):
        for m in range(1 + i):
            keep_total(i, m).wait()
            if whole_plane:
                spread_2(i, m, 0).wait_recv()
                spread_2(i, m, 1).wait_recv()
                spread_3(i, m).start()

    ids_copy = remote(ids_in, ids.at[c], pair(s_ids), dev_core)
    ids_copy.start()
    own = [
        pltpu.make_async_copy(shard_qkv, w_att.at[0, pl.ds(0, 3)], s_loc.at[0]),
        pltpu.make_async_copy(shard_out, w_att.at[0, 3], s_loc.at[3]),
        pltpu.make_async_copy(shard_up, w_ffn.at[0, :, :, 0], s_loc.at[1]),
        pltpu.make_async_copy(shard_down, w_ffn.at[0, :, :, 1], s_loc.at[2]),
    ]
    for copy in own:
        copy.start()
    own_piece = (w_att.at[0, yx, c], w_ffn.at[0, yx, c])
    bias[0, 0:1, :] = bias_up[...][None]
    bias[0, 1:2, :part] = bias_qv[0:1]
    bias[0, 1:2, part : 2 * part] = bias_qv[1:2]
    bias[0, 1:2, 2 * part :] = jnp.zeros((1, width - 2 * part), F32)

    def bias_copy(s):
        line = source[s]
        slot = (0, by_line(2, 2, 1, 1), by_line(3, 1, 1, 3), by_line(3, 2, 2, 3))[s]
        return remote(bias.at[0], bias.at[slot], (s_bias.at[0, s], s_bias.at[1, slot]), at(d, line))

    def bias_got(s):
        remote(bias.at[s], bias.at[s], (s_bias.at[0, s], s_bias.at[1, s]), dev_core).wait_recv()

    for s in range(1, lines):
        bias_copy(s).start()
    ids[pl.ds(c, 1)] = ids_in[...][None]

    def see():
        remote(ids_in, ids.at[1 - c], pair(s_ids), dev_core).wait_recv()
        row = ids[t // 2, pl.ds(lax.rem(t, 2), 1), :].astype(F32)
        low, high = row[:, :half], row[:, half:]
        first_core = c == 0
        ids_own = jnp.where(first_core, low, high)
        ids_other = jnp.where(first_core, high, low)
        for place, ids_k in enumerate((ids_own, ids_other)):
            columns = jnp.broadcast_to(ids_k, (128, half)).T
            for j in range(0, half, 128):
                mask[place, :, j : j + 128] = jnp.where(columns == ids_own[:, j : j + 128], 0.0, -1e30)

    def att_weights(s):
        return w_att[s].reshape(width, width)

    def up_weights(s):
        return w_ffn[s, :, :, 0].reshape(width, width)

    def down_weights(s):
        return w_ffn[s, :, :, 1].reshape(width, width)

    def kv_copy(s):
        return remote(kv.at[s], kvs.at[s], pair(s_kv, s), dev_core)

    def project(s):
        qkv = dot(att_weights(s)[: 3 * part], n1[...], NT)
        bias_row = bias[s, 1:2, : 2 * part]
        bias_col = jnp.broadcast_to(bias_row, (128, 2 * part)).T[:, :1]
        qt[s] = (qkv[:part] + bias_col[:part]).astype(BF)
        kv[s, 0] = qkv[part : 2 * part].astype(BF)
        kv[s, 1] = (qkv[2 * part :] + bias_col[part:]).astype(BF)
        kv_copy(s).start()

    def kvg_copy(s):
        return remote(kvs.at[s], kvg.at[s], pair(s_kvg, s), dev_core)

    def finish(s):
        kvg_copy(s).wait_recv()
        dq = qt[s]
        dkv = (kv[s].astype(F32) + kvg[s].astype(F32)).astype(BF).reshape(2 * part, half)
        ones = jnp.ones((8, half), BF)
        sums[s, 1:2, :part] = dot(ones, dq, NT)[:1]
        sums[s, 1:2, part : 2 * part] = dot(ones, dkv[part:], NT)[:1]
        sums[s, 1:2, 2 * part :] = jnp.zeros((1, width - 2 * part), F32)
        stacked = jnp.concatenate([dq, dkv], axis=0)
        acc[...] += dot(stacked, att_weights(s)[: 3 * part], TN)
        w_att[s, 0:3] = dot(stacked, n1[...], NN).astype(BF).reshape(3, 2, 96, width)
        fold_1(ATT, s)

    def sums_copy(s):
        return remote(
            sums.at[s],
            sums_z.at[t],
            (s_sz.at[0, s], s_sz.at[1, t]),
            at(d, source[s]),
        )

    def sums_got(s):
        ref = sums_z.at[source[s]]
        remote(ref, ref, (s_sz.at[0, s], s_sz.at[1, source[s]]), dev_core).wait_recv()

    dev_x = at(base + 2 * yx_x + c, t)
    dev_y = at(base + 2 * yx_y + c, t)

    def flip(k):
        return remote(
            sums_p.at[2 * k], sums_p.at[2 * k + 1], pair(s_sp, k), (dev_core, dev_x, dev_y)[k]
        )

    def sums_start():
        for s in range(1, lines):
            sums_copy(s).start()
        sums_z[pl.ds(t, 1)] = sums[0:1]

    def sums_line():
        for s in range(1, lines):
            sums_got(s)
        sums_p[0] = (sums_z[0] + sums_z[1]) + (sums_z[2] + sums_z[3])
        flip(0).start()

    def sums_plane(k):
        flip(k - 1).wait()
        sums_p[2 * k] = sums_p[2 * k - 2] + sums_p[2 * k - 1]
        flip(k).start()

    def sums_end():
        flip(2).wait()
        small_out[...] = sums_p[4] + sums_p[5]

    steps = {
        Z_OWN: z_own,
        Z_PASS: z_pass,
        STEP_1: step_1,
        STEP_2: step_2,
        STEP_3: step_3,
        FOLD_2: fold_2,
        FOLD_3: fold_3,
        FOLD_4: fold_4,
        FOLD_5: fold_5,
        TOTAL: total,
        SPREAD_2: spread_step_2,
        SPREAD_3: spread_step_3,
        FINISH: finish,
        SEE: see,
        SUMS: sums_start,
        SUMS_Z: sums_line,
        SUMS_P: sums_plane,
        SUMS_END: sums_end,
        MOVE: lambda name, *which: to_owner(*rows[name], *which),
    }
    rows = {
        X: (tokens, xb, s_x),
        G: (cotangent, gb, s_g),
        BO: (bo, block_home, s_bo),
        IG: (ig, input_home, s_ig),
    }

    def run(*where):
        for name, *which in PLAN.get(where, ()):
            steps[name](*which)

    def point(loop, j, where):
        for k in range(lines):
            if (loop, k, where) in PLAN:
                pl.when(j == k)(functools.partial(run, loop, k, where))

    run(START)
    to_owner_wait(tokens, xb, s_x)
    run(X_HERE)
    normed, _ = norm_parts(xb[...].reshape(half, width).astype(F32))
    n1[...] = (normed * gain_first + shift_first).astype(BF)
    for s in range(1, lines):
        bias_got(s)
    project(0)
    run(FIRST)

    def attend(s, carry):
        @pl.when(s < lines - 1)
        def _():
            step_4(ATT, s + 1)
            project(s + 1)

        kv_copy(s).wait_recv()
        for h in range(part // HEAD):
            rows = slice(h * HEAD, (h + 1) * HEAD)
            q = qt[s, rows, :]
            s0 = dot(kv[s, 0, rows, :].T, q, NN) * FACTOR + mask[0]
            s1 = dot(kvs[s, 0, rows, :].T, q, NN) * FACTOR + mask[1]
            top = jnp.maximum(
                jnp.max(s0, axis=0, keepdims=True), jnp.max(s1, axis=0, keepdims=True)
            )
            p0 = jnp.exp2(s0 - top)
            p1 = jnp.exp2(s1 - top)
            weight = column_sum(p0) + column_sum(p1)
            out = dot(kv[s, 1, rows, :], p0.astype(BF), NN)
            out = out + dot(kvs[s, 1, rows, :], p1.astype(BF), NN)
            ct[s, rows, :] = (out / weight).astype(BF)
            lse[s, h : h + 1, :] = top + jnp.log2(weight)
            point(ATTEND, s, h)
        return carry

    lax.fori_loop(0, lines, attend, 0)

    mid = xb[...].reshape(half, width).astype(F32) + bias_out
    for s in range(lines):
        mid = mid + dot(ct[s], att_weights(s)[3 * part :], TN)
    middle[...] = mid
    normed, _ = norm_parts(mid)
    low_normed = (normed * gain_second + shift_second).astype(BF)
    n2[...] = low_normed
    n2t[...] = low_normed.T
    acc[...] = mid + bias_down
    acc2[...] = jnp.zeros_like(acc2)
    run(OUT)
    to_owner_wait(cotangent, gb, s_g)

    def feed(s, carry):
        @pl.when(s > 0)
        def _():
            step_4(FFN, s)

        for k in range(lines):
            pl.when(s == k)(functools.partial(z_sent, FFN, k))
        point(FEED, s, 0)
        grad = gb[...].reshape(half, width)
        pre = dot(n2[...], up_weights(s), NN) + bias[s, 0:1, :]
        phi = 0.5 * (1.0 + lax.erf(pre * 0.7071067811865476))
        active = (pre * phi).astype(BF)
        slope = phi + pre * jnp.exp(-0.5 * pre * pre) * 0.3989422804014327
        acc[...] += dot(active, down_weights(s), NN)
        point(FEED, s, 1)
        pre_grad = (dot(grad, down_weights(s), NT) * slope).astype(BF)
        sums[s, 0:1, :] = dot(jnp.ones((8, half), BF), pre_grad, NN)[:1]
        point(FEED, s, 2)
        acc2[...] += dot(pre_grad, up_weights(s), NT)
        point(FEED, s, 3)
        w_ffn[s, :, :, 1] = dot(active, grad, TN).astype(BF).reshape(4, 2, 96, width)
        point(FEED, s, 4)
        w_ffn[s, :, :, 0] = dot(n2t[...], pre_grad, NN).astype(BF).reshape(4, 2, 96, width)
        fold_1(FFN, s)
        point(FEED, s, 5)
        return carry

    lax.fori_loop(0, lines, feed, 0)

    mid = middle[...]
    bo[...] = acc[...].astype(BF).reshape(2, 256, width)
    run(BLOCK)
    normed, rate = norm_parts(mid)
    grad = gb[...].reshape(half, width).astype(F32)
    back = acc2[...]
    middle_grad = grad + norm_back(normed, rate, back, gain_second)
    vec_out = column_sum(middle_grad)
    vec_gain = column_sum(back * normed)
    vec_shift = column_sum(back)
    vec_down = column_sum(grad)
    for s in range(lines):
        sums[s, 4:5, :] = vec_out
        sums[s, 5:6, :] = vec_gain
        sums[s, 6:7, :] = vec_shift
        sums[s, 7:8, :] = vec_down
    acc2[...] = middle_grad
    dmr[...] = middle_grad.astype(BF)
    acc[...] = jnp.zeros_like(acc)
    for s in range(lines):
        z_sent(ATT, s)
    run(NORM)

    def attend_back(j, carry):
        s = by_line_of(j, *ORDER)
        dct = dot(w_att[s, 3].reshape(part, width), dmr[...], NT).astype(BF)
        w_att[s, 3] = dot(ct[s], dmr[...], NN).astype(BF).reshape(2, 96, width)
        kv_copy(s).wait_send()
        point(BACK, j, 0)
        for h in range(part // HEAD):
            rows = slice(h * HEAD, (h + 1) * HEAD)
            g = dct[rows]
            q = qt[s, rows, :]
            along = column_sum(g.astype(F32) * ct[s, rows, :].astype(F32))
            total_log = lse[s, h : h + 1, :]
            dq = jnp.zeros((HEAD, half), F32)
            for place, ref in enumerate((kv, kvs)):
                k = ref[s, 0, rows, :]
                v = ref[s, 1, rows, :]
                p = jnp.exp2(dot(k.T, q, NN) * FACTOR + mask[place] - total_log)
                ds = (p * (dot(v.T, g, NN) - along)).astype(BF)
                ref[s, 0, rows, :] = (dot(q, ds, NT) * HEAD**-0.5).astype(BF)
                ref[s, 1, rows, :] = dot(g, p.astype(BF), NT).astype(BF)
                dq = dq + dot(k, ds, NN)
            qt[s, rows, :] = (dq * HEAD**-0.5).astype(BF)
            if h == part // HEAD - 1:
                kvg_copy(s).start()
            point(BACK, j, h + 1)
        return carry

    lax.fori_loop(0, lines, attend_back, 0)
    run(TAIL_0)

    normed, rate = norm_parts(xb[...].reshape(half, width).astype(F32))
    back = acc[...]
    vec_gain = column_sum(back * normed)
    vec_shift = column_sum(back)
    for s in range(lines):
        sums[s, 2:3, :] = vec_gain
        sums[s, 3:4, :] = vec_shift

    run(TAIL_1)
    ig[...] = (
        (acc2[...] + norm_back(normed, rate, back, gain_first))
        .astype(BF)
        .reshape(2, 256, width)
    )
    run(TAIL_2)
    run(TAIL_3)

    ids_copy.wait_send()
    for s in range(1, lines):
        bias_copy(s).wait_send()
        sums_copy(s).wait_send()
    to_owner_sent(tokens, s_x)
    to_owner_sent(cotangent, s_g)
    to_owner_wait(bo, block_home, s_bo)
    to_owner_sent(bo, s_bo)
    for s in range(lines):
        kvg_copy(s).wait_send()
    for i in (ATT, FFN):
        for s in range(lines):
            reduce_core(i, s).wait_send()
            reduce_a(i, s, 0).wait_send()
            reduce_a(i, s, 1).wait_send()
            reduce_b(i, s).wait_send()
            if s > 0:
                reduce_z(i, s).wait_send()
        for m in range(1 + i if whole_plane else 0):
            spread_1(i, m).wait_send()
            spread_2(i, m, 0).wait_send()
            spread_2(i, m, 1).wait_send()
            spread_3(i, m).wait()
    to_owner_wait(ig, input_home, s_ig)
    to_owner_sent(ig, s_ig)


def layer(lines, whole_plane, operands):
    def dma(*shape):
        return pltpu.SemaphoreType.DMA((2,) + shape)

    def vmem(*shape, dtype=BF):
        return pltpu.VMEM(shape, dtype)

    n = lines
    anywhere = pl.BlockSpec(memory_space=pl.ANY)
    inside = pl.BlockSpec(memory_space=pltpu.VMEM)
    att = (96, 768)
    ffn = (2, 96, 768)
    plane = (4, 2) if whole_plane else ()
    blocks = jax.ShapeDtypeStruct((2, 256, 768), BF)
    return pl.pallas_call(
        functools.partial(layer_kernel, lines, whole_plane),
        in_specs=[anywhere, anywhere, inside] + [anywhere] * 4 + [inside] * 8,
        out_specs=[anywhere] * 5 + [inside],
        out_shape=[
            blocks,
            blocks,
            jax.ShapeDtypeStruct(plane + att, BF),
            jax.ShapeDtypeStruct(plane + att, BF),
            jax.ShapeDtypeStruct(plane + att, BF),
            jax.ShapeDtypeStruct((8, 768), F32),
        ],
        scratch_shapes=[
            vmem(n, 4, 2, *att),
            vmem(n, 4, 2, *ffn),
            vmem(n, 4, *att),
            vmem(n, 4, *ffn),
            vmem(n, 2, *att),
            vmem(n, 2, *ffn),
            vmem(n, *att),
            vmem(n, *ffn),
            vmem(5, *att),
            vmem(5, *ffn),
            vmem(2, 256, 768),
            vmem(2, 256, 768),
            vmem(2, 2, 1024, dtype=jnp.int32),
            vmem(n, 8, 768, dtype=F32),
            vmem(2, 512, 512, dtype=F32),
            vmem(512, 768),
            vmem(512, 768),
            vmem(768, 512),
            vmem(512, 768, dtype=F32),
            vmem(512, 768, dtype=F32),
            vmem(512, 768, dtype=F32),
            vmem(512, 768),
            vmem(n, 192, 512),
            vmem(n, 2, 192, 512),
            vmem(n, 2, 192, 512),
            vmem(n, 2, 192, 512),
            vmem(n, 192, 512),
            vmem(n, 8, 512, dtype=F32),
            vmem(2, 256, 768),
            vmem(2, 256, 768),
            vmem(n, 8, 768, dtype=F32),
            vmem(n, 8, 768, dtype=F32),
            vmem(6, 8, 768, dtype=F32),
            pltpu.SemaphoreType.DMA((7,)),
            dma(),
            dma(n),
            dma(2, 2),
            dma(2, 2),
            dma(2, 2),
            dma(2, 2),
            dma(n),
            dma(n),
            pltpu.SemaphoreType.DMA((2, 5)),
            pltpu.SemaphoreType.DMA((2, n)),
            dma(2, n - 1),
            dma(2, n - 1, 2),
            dma(2, n - 1),
            dma(2, n),
            dma(2, n, 2),
            dma(2, n),
            pltpu.SemaphoreType.DMA((2, n)),
            pltpu.SemaphoreType.DMA((2, 5)),
            dma(3),
            dma(3, 2),
            dma(3),
            dma(n),
            dma(3),
        ],
        compiler_params=pltpu.CompilerParams(
            collective_id=0, has_side_effects=True, vmem_limit_bytes=62 * 2**20
        ),
        name="layer",
    )(*operands)


def results_kernel(
    block_in, input_in, att_in, up_in, down_in, small_in,
    block_out, input_out, qkv_out, out_out, up_out, down_out, bias_out, *rest
):
    sums_out, (low_in, low_att, low_up, low_down) = rest[:7], rest[7:11]
    wide_in, wide_att, wide_up, wide_down, low_block, s_in, s_out, s_block = rest[11:]
    part = bias_out.shape[1]
    third = 3 * part
    block = pltpu.make_async_copy(block_in, low_block, s_block)
    jobs = [(up_in, low_up, wide_up, up_out, 0, 0, 2 * part)]
    jobs += [(up_in, low_up, wide_up, up_out, 2 * part, 2 * part, 2 * part)]
    jobs += [(down_in, low_down, wide_down, down_out, k, k, 2 * part) for k in (0, 2 * part)]
    jobs += [(att_in, low_att, wide_att, qkv_out, 0, 0, third)]
    jobs += [(att_in, low_att, wide_att, out_out, third, 0, part)]
    jobs += [(input_in, low_in, wide_in, input_out, k, k, 256) for k in (0, 256)]

    def fetch(k):
        source, low, _, _, at, _, size = jobs[k]
        rows = pl.ds(at, size)
        return pltpu.make_async_copy(source.at[rows], low.at[rows], s_in.at[k])

    def store(k):
        _, _, wide, result, at, to, size = jobs[k]
        return pltpu.make_async_copy(wide.at[pl.ds(at, size)], result.at[pl.ds(to, size)], s_out.at[k])

    for k in range(len(jobs)):
        fetch(k).start()
    block.start()
    bias_out[0:1] = small_in[1:2, :part]
    bias_out[1:2] = small_in[1:2, part : 2 * part]
    for ref, row in zip(sums_out, (0, 2, 3, 4, 5, 6, 7)):
        ref[...] = small_in[row]
    for k, (_, low, wide, _, at, _, size) in enumerate(jobs):
        fetch(k).wait()
        wide[pl.ds(at, size)] = low[pl.ds(at, size)].astype(F32)
        store(k).start()
    block.wait()
    block = pltpu.make_async_copy(low_block, block_out, s_block)
    block.start()
    for k in range(len(jobs)):
        store(k).wait()
    block.wait()


def results(block, inputs, att, up, down, small):
    width = att.shape[0]
    part = width // 4
    tokens = inputs.shape[0] * inputs.shape[1]
    anywhere = pl.BlockSpec(memory_space=pl.ANY)
    inside = pl.BlockSpec(memory_space=pltpu.VMEM)
    shapes = ((tokens, width), (width, width), (width, width), (width, width))
    block, inputs, *results = pl.pallas_call(
        results_kernel,
        in_specs=[anywhere] * 5 + [inside],
        out_specs=[anywhere] * 6 + [inside] * 8,
        out_shape=[
            jax.ShapeDtypeStruct(block.shape, BF),
            jax.ShapeDtypeStruct((tokens, width), F32),
            jax.ShapeDtypeStruct((3 * part, width), F32),
            jax.ShapeDtypeStruct((part, width), F32),
            jax.ShapeDtypeStruct((width, width), F32),
            jax.ShapeDtypeStruct((width, width), F32),
            jax.ShapeDtypeStruct((2, part), F32),
        ]
        + [jax.ShapeDtypeStruct((width,), F32)] * 7,
        scratch_shapes=[pltpu.VMEM(shape, BF) for shape in shapes]
        + [pltpu.VMEM(shape, F32) for shape in shapes]
        + [pltpu.VMEM(block.shape, BF)]
        + [pltpu.SemaphoreType.DMA((8,)), pltpu.SemaphoreType.DMA((8,)), pltpu.SemaphoreType.DMA],
        compiler_params=pltpu.CompilerParams(vmem_limit_bytes=62 * 2**20),
        name="results",
    )(block, inputs.reshape(tokens, width), att, up, down, small)
    return (block, inputs.reshape(block.shape), *results)


def body(
    dp,
    lines,
    tokens,
    segment_ids,
    gain_first,
    shift_first,
    weight_qkv,
    bias_qv,
    weight_out,
    bias_out,
    gain_second,
    shift_second,
    weight_up,
    bias_up,
    weight_down,
    bias_down,
    cotangent,
):
    width = tokens.shape[2]
    part = weight_qkv.shape[2]
    shard = (4, 2, width // PLANE, width)
    whole_plane = dp == PLANE
    block_out, input_grad, *grads, small = layer(
        lines,
        whole_plane,
        (
            tokens,
            cotangent,
            segment_ids,
            weight_qkv.reshape(width, 3 * part).T.reshape(3, 2, width // PLANE, width),
            weight_out.reshape(2, width // PLANE, width),
            weight_up.reshape(shard),
            weight_down.reshape(shard),
            bias_up,
            bias_qv,
            gain_first,
            shift_first,
            bias_out,
            gain_second,
            shift_second,
            bias_down,
        ),
    )
    if not whole_plane:
        apart = [[i + PLANE * g for g in range(dp // PLANE)] for i in range(PLANE)]
        planes = [[i + PLANE * g for i in range(PLANE)] for g in range(dp // PLANE)]
        sums = tuple(grad.astype(F32) for grad in grads)
        *grads, small = lax.psum(sums + (small,), "dp", axis_index_groups=apart)
        grads = [lax.all_gather(g.astype(BF), "dp", axis_index_groups=planes) for g in grads]
    att_grad, up_grad, down_grad = [grad.reshape(width, width) for grad in grads]
    block_out, input_grad, qkv_grad, out_grad, up_grad, down_grad, bias_grad, *sums = results(
        block_out, input_grad, att_grad, up_grad, down_grad, small
    )
    up_bias, gain_one, shift_one, out_bias, gain_two, shift_two, down_bias = sums
    return (
        block_out,
        input_grad,
        gain_one,
        shift_one,
        qkv_grad.T.reshape(width, 3, part),
        bias_grad,
        out_grad,
        out_bias,
        gain_two,
        shift_two,
        up_grad,
        up_bias,
        down_grad,
        down_bias,
    )


def solution(mesh):
    in_specs = (
        P("dp", "tensor", None),
        P("dp", None),
        P(),
        P(),
        P(None, None, "tensor"),
        P(None, "tensor"),
        P("tensor", None),
        P(),
        P(),
        P(),
        P(None, "tensor"),
        P("tensor"),
        P("tensor", None),
        P(),
        P("dp", "tensor", None),
    )
    out_specs = (
        P("dp", "tensor", None),
        P("dp", "tensor", None),
        P(),
        P(),
        P(None, None, "tensor"),
        P(None, "tensor"),
        P("tensor", None),
        P(),
        P(),
        P(),
        P(None, "tensor"),
        P("tensor"),
        P("tensor", None),
        P(),
    )
    whole = functools.partial(body, mesh.shape["dp"], mesh.shape["tensor"])
    return jax.shard_map(whole, mesh=mesh, in_specs=in_specs, out_specs=out_specs, check_vma=False)
```
